512 devices in a mesh: sec: 8 (over z_hi, x), gy: 8 (over z_lo, core), gx: 8 (over y).
Axes of the slice: x: 4, y: 8, z: 8 (z_hi: 2, z_lo: 4; z = z_hi * 4 + z_lo), core: 2. Of those that a mesh axis runs over, the one named last changes fastest.
Arguments:
- images: bfloat16 [64, 64, 1024], P(('sec', 'gy'), None, 'gx'), may hold values from -6 to 6
- offsets: int32 [64, 8, 2, 8], P(('sec', 'gy'), None, None, 'gx'), may hold values from 0 to 4, as said below
- stem_kernel: bfloat16 [32, 1, 1, 3, 3], replicated, may hold values from -2 to 2
- stem_bias: float32 [32], replicated, may hold values from -3 to 3
- outer_kernel: bfloat16 [32, 32, 1, 3, 3], replicated, may hold values from -0.375 to 0.375
- outer_bias: float32 [32], replicated, may hold values from -3 to 3
- pooling_kernel: bfloat16 [64, 32, 1, 2, 2], replicated, may hold values from -0.5 to 0.5
- pooling_bias: float32 [64], replicated, may hold values from -3 to 3
- inner_kernel: bfloat16 [3, 3, 3, 4096], replicated, may hold values from -0.15625 to 0.15625
- inner_bias: float32 [64], replicated, may hold values from -3 to 3
- narrowing_kernel: bfloat16 [128, 64, 1, 2, 2], replicated, may hold values from -0.375 to 0.375
- narrowing_bias: float32 [128], replicated, may hold values from -3 to 3
- bottom_kernel: bfloat16 [3, 3, 3, 16384], replicated, may hold values from -0.109375 to 0.109375
- bottom_bias: float32 [128], replicated, may hold values from -3 to 3
- lift_kernel: bfloat16 [128, 64, 1, 2, 2], replicated, may hold values from -0.5 to 0.5
- lift_bias: float32 [64], replicated, may hold values from -3 to 3
- mend_kernel: bfloat16 [64, 64, 1, 3, 3], replicated, may hold values from -0.25 to 0.25
- mend_bias: float32 [64], replicated, may hold values from -3 to 3
- expand_kernel: bfloat16 [64, 32, 1, 2, 2], replicated, may hold values from -0.75 to 0.75
- expand_bias: float32 [32], replicated, may hold values from -3 to 3
- finish_kernel: bfloat16 [32, 32, 1, 3, 3], replicated, may hold values from -0.375 to 0.375
- finish_bias: float32 [32], replicated, may hold values from -3 to 3
- head_kernel: bfloat16 [3, 32], replicated, may hold values from -1 to 1
- head_bias: float32 [3], replicated, may hold values from -3 to 3
Outputs:
- affinities: float32 [3, 64, 64, 1024], P(None, 'sec', 'gy', 'gx')
The draws below stay inside these ranges and needn't reach their ends.
Inputs may be any that keep to these rules, and one draw needn't show every extreme that they name: `offsets`: each section has a tile with a shift of exactly 4.
All inputs are finite; a program needn't handle non-finite values.
Results may differ from the reference program's by a relative error of at most 0.025.
Values may be sent and summed in bfloat16 or wider, within the bound.
A program may use at most 64 MiB of HBM per device.

```python
import jax
import jax.numpy as jnp
from jax import lax

ROW_DEV = 8
COL_DEV = 128
MAX_SHIFT = 4
CH0 = 32
CH1 = 64
CH2 = 128
SECTIONS = 64
ROWS = 64
COLS = 1024
TILE_ROWS = 8
TILE_COLS = 8


def draw_offsets(key, part):
    key = jax.random.fold_in(key, 11)
    key_values, key_chosen = jax.random.split(key)
    entries = TILE_ROWS * 2 * TILE_COLS
    values = jax.random.randint(key_values, (SECTIONS, TILE_ROWS, 2, TILE_COLS), 0, MAX_SHIFT + 1)
    chosen = jax.random.randint(key_chosen, (SECTIONS, 1, 1, 1), 0, entries)
    position = jnp.arange(entries, dtype=jnp.int32).reshape(1, TILE_ROWS, 2, TILE_COLS)
    return jnp.where(position == chosen, MAX_SHIFT, values).astype(jnp.int32)


def block_levels(key, shape, cuts, smallest, largest):
    def one(axis_at, blocks):
        draws = jax.random.uniform(jax.random.fold_in(jax.random.fold_in(key, 6), axis_at), (blocks,), jnp.float32, smallest / len(cuts), largest / len(cuts))
        return jnp.repeat(jnp.exp(draws), shape[axis_at] // blocks).reshape((-1,) + (1,) * (len(shape) - axis_at - 1))

    factor_of = one(*cuts[0])
    for cut in cuts[1:]:
        factor_of = factor_of * one(*cut)
    return factor_of


def gaussian(own_key, dims, deviation, most, cuts=(), kind=jnp.bfloat16):
    values = jax.random.normal(own_key, dims, jnp.float32) * deviation
    if len(cuts) > 0:
        values = block_levels(own_key, dims, cuts, -0.22, 0.18) * values
    return jnp.clip(values, min=-most, max=most).astype(kind)


def setup_inputs(seed: int = 0) -> dict:
    key_of = jax.random.split(jax.random.key(seed), 25)
    images = gaussian(key_of[0], (SECTIONS, ROWS, COLS), 1.0, 6.0, ((0, 64), (2, 8)))
    offsets = draw_offsets(jax.random.fold_in(key_of[24], 71), 0)
    stem_kernel = gaussian(key_of[2], (CH0, 1, 1, 3, 3), 9 ** -0.5, 2.0)
    stem_bias = gaussian(key_of[3], (CH0,), 0.5, 3.0, (), jnp.float32)
    outer_kernel = gaussian(key_of[4], (CH0, CH0, 1, 3, 3), (9 * CH0) ** -0.5, 0.375)
    outer_bias = gaussian(key_of[5], (CH0,), 0.5, 3.0, (), jnp.float32)
    pooling_kernel = gaussian(key_of[6], (CH1, CH0, 1, 2, 2), (4 * CH0) ** -0.5, 0.5)
    pooling_bias = gaussian(key_of[7], (CH1,), 0.5, 3.0, (), jnp.float32)
    inner_kernel = gaussian(key_of[8], (3, 3, 3, CH1 * CH1), (27 * CH1) ** -0.5, 0.15625)
    inner_bias = gaussian(key_of[9], (CH1,), 0.5, 3.0, (), jnp.float32)
    narrowing_kernel = gaussian(key_of[10], (CH2, CH1, 1, 2, 2), (4 * CH1) ** -0.5, 0.375)
    narrowing_bias = gaussian(key_of[11], (CH2,), 0.5, 3.0, (), jnp.float32)
    bottom_kernel = gaussian(key_of[12], (3, 3, 3, CH2 * CH2), (27 * CH2) ** -0.5, 0.109375)
    bottom_bias = gaussian(key_of[13], (CH2,), 0.5, 3.0, (), jnp.float32)
    lift_kernel = gaussian(key_of[14], (CH2, CH1, 1, 2, 2), CH2 ** -0.5, 0.5)
    lift_bias = gaussian(key_of[15], (CH1,), 0.5, 3.0, (), jnp.float32)
    mend_kernel = gaussian(key_of[16], (CH1, CH1, 1, 3, 3), (9 * CH1) ** -0.5, 0.25)
    mend_bias = gaussian(key_of[17], (CH1,), 0.5, 3.0, (), jnp.float32)
    expand_kernel = gaussian(key_of[18], (CH1, CH0, 1, 2, 2), CH1 ** -0.5, 0.75)
    expand_bias = gaussian(key_of[19], (CH0,), 0.5, 3.0, (), jnp.float32)
    finish_kernel = gaussian(key_of[20], (CH0, CH0, 1, 3, 3), (9 * CH0) ** -0.5, 0.375)
    finish_bias = gaussian(key_of[21], (CH0,), 0.5, 3.0, (), jnp.float32)
    head_kernel = gaussian(key_of[22], (3, CH0), CH0 ** -0.5, 1.0)
    head_bias = gaussian(key_of[23], (3,), 0.5, 3.0, (), jnp.float32)
    return {"images": images, "offsets": offsets, "stem_kernel": stem_kernel, "stem_bias": stem_bias, "outer_kernel": outer_kernel, "outer_bias": outer_bias, "pooling_kernel": pooling_kernel, "pooling_bias": pooling_bias, "inner_kernel": inner_kernel, "inner_bias": inner_bias, "narrowing_kernel": narrowing_kernel, "narrowing_bias": narrowing_bias, "bottom_kernel": bottom_kernel, "bottom_bias": bottom_bias, "lift_kernel": lift_kernel, "lift_bias": lift_bias, "mend_kernel": mend_kernel, "mend_bias": mend_bias, "expand_kernel": expand_kernel, "expand_bias": expand_bias, "finish_kernel": finish_kernel, "finish_bias": finish_bias, "head_kernel": head_kernel, "head_bias": head_bias}


LAYOUT = ("NCDHW", "OIDHW", "NCDHW")
HIGHEST = lax.Precision.HIGHEST
PLANE_PAD = ((0, 0), (1, 1), (1, 1))
CUBE_PAD = ((1, 1), (1, 1), (1, 1))
NO_PAD = ((0, 0), (0, 0), (0, 0))


def unfold_kernel(kernel_weight):
    channels = math_root(kernel_weight.shape[3])
    return kernel_weight.reshape(3, 3, 3, channels, channels).transpose(4, 3, 0, 1, 2)


def math_root(count):
    width = 1
    while width * width < count:
        width = width + 1
    return width


def lag_one(array, axis):
    widths = [(0, 0)] * array.ndim
    widths[axis] = (1, 0)
    padded = jnp.pad(array, widths)
    return lax.slice_in_dim(padded, 0, array.shape[axis], axis=axis)


def place_tiles(source, row_start, col_start, out_rows, out_cols):
    source_rows = jnp.arange(source.shape[1], dtype=jnp.int32)
    source_cols = jnp.arange(source.shape[2], dtype=jnp.int32)
    dest_rows = jnp.arange(out_rows, dtype=jnp.int32)
    dest_cols = jnp.arange(out_cols, dtype=jnp.int32)
    row_pick = (source_rows[None, None, :] == dest_rows[None, :, None] - row_start[:, None, None]).astype(jnp.float32)
    col_pick = (source_cols[None, :, None] == dest_cols[None, None, :] - col_start[:, None, None]).astype(jnp.float32)
    partial_rows = jnp.einsum("bar,brc->bac", row_pick, source.astype(jnp.float32), precision=HIGHEST)
    placed = jnp.einsum("bac,bcx->bax", partial_rows, col_pick, precision=HIGHEST)
    covered = jnp.sum(row_pick, axis=2)[:, :, None] * jnp.sum(col_pick, axis=1)[:, None, :]
    return placed, covered


def align_tiles(own, upper, left_rim, corner, own_shift, upper_shift, left_shift, corner_shift):
    margin = MAX_SHIFT
    sources = ((own, own_shift[:, 0], own_shift[:, 1]),
               (upper, upper_shift[:, 0] - margin, upper_shift[:, 1]),
               (left_rim, left_shift[:, 0], left_shift[:, 1] - margin),
               (corner, corner_shift[:, 0] - margin, corner_shift[:, 1] - margin))
    total = jnp.zeros(own.shape, jnp.float32)
    cover = jnp.zeros(own.shape, jnp.float32)
    for source, row_start, col_start in sources:
        placed, covered = place_tiles(source, row_start, col_start, own.shape[1], own.shape[2])
        total = total + placed
        cover = cover + covered
    return (total / jnp.maximum(cover, 1.0)).astype(jnp.bfloat16)


def tile_batch(array):
    return array.reshape((-1,) + array.shape[3:])


def align_volume(images, offsets):
    margin = MAX_SHIFT
    grid = images.reshape(SECTIONS, TILE_ROWS, ROW_DEV, TILE_COLS, COL_DEV).transpose(0, 1, 3, 2, 4)
    shifts = offsets.transpose(0, 1, 3, 2)
    upper = lag_one(grid[:, :, :, ROW_DEV - margin:, :], 1)
    left_rim = lag_one(grid[:, :, :, :, COL_DEV - margin:], 2)
    corner = lag_one(lag_one(grid[:, :, :, ROW_DEV - margin:, COL_DEV - margin:], 1), 2)
    upper_shift = lag_one(shifts, 1)
    left_shift = lag_one(shifts, 2)
    corner_shift = lag_one(lag_one(shifts, 1), 2)
    aligned_tiles = align_tiles(tile_batch(grid), tile_batch(upper), tile_batch(left_rim), tile_batch(corner),
                                tile_batch(shifts), tile_batch(upper_shift), tile_batch(left_shift), tile_batch(corner_shift))
    aligned_tiles = aligned_tiles.reshape(SECTIONS, TILE_ROWS, TILE_COLS, ROW_DEV, COL_DEV)
    return aligned_tiles.transpose(0, 1, 3, 2, 4).reshape(SECTIONS, ROWS, COLS)


def conv_apply(feature_maps, kernel_weight, strides, padding, dilation):
    result = lax.conv_general_dilated(feature_maps.astype(jnp.float32)[None], kernel_weight.astype(jnp.float32), strides, padding,
                                      lhs_dilation=dilation, dimension_numbers=LAYOUT, precision=HIGHEST)
    return result[0]


def with_bias(result, bias_terms):
    return result + bias_terms.astype(jnp.float32)[:, None, None, None]


def residual(feature_maps, kernel_weight, bias_terms, padding):
    branch = conv_apply(jax.nn.relu(feature_maps), kernel_weight, (1, 1, 1), padding, (1, 1, 1))
    return with_bias(feature_maps.astype(jnp.float32) + branch, bias_terms).astype(jnp.bfloat16)


def reduce_resolution(feature_maps, kernel_weight, bias_terms):
    return with_bias(conv_apply(feature_maps, kernel_weight, (1, 2, 2), NO_PAD, (1, 1, 1)), bias_terms).astype(jnp.bfloat16)


def upsample(feature_maps, kernel_weight, bias_terms, skipped):
    flipped = jnp.flip(kernel_weight, axis=(3, 4)).transpose(1, 0, 2, 3, 4)
    result = conv_apply(feature_maps, flipped, (1, 1, 1), PLANE_PAD, (1, 2, 2))
    return with_bias(result + skipped.astype(jnp.float32), bias_terms).astype(jnp.bfloat16)


def reference(images, offsets, stem_kernel, stem_bias, outer_kernel, outer_bias, pooling_kernel, pooling_bias,
              inner_kernel, inner_bias, narrowing_kernel, narrowing_bias, bottom_kernel, bottom_bias,
              lift_kernel, lift_bias, mend_kernel, mend_bias, expand_kernel, expand_bias,
              finish_kernel, finish_bias, head_kernel, head_bias):
    aligned = align_volume(images, offsets)
    inner_full = unfold_kernel(inner_kernel)
    bottom_full = unfold_kernel(bottom_kernel)

    def encode(section):
        plane_image = section[None, None]
        stem_act = with_bias(conv_apply(plane_image, stem_kernel, (1, 1, 1), PLANE_PAD, (1, 1, 1)), stem_bias).astype(jnp.bfloat16)
        outer_activation = residual(stem_act, outer_kernel, outer_bias, PLANE_PAD)
        pooled_maps = reduce_resolution(outer_activation, pooling_kernel, pooling_bias)
        return outer_activation[:, 0], pooled_maps[:, 0]

    outer_all, pooled_all = lax.map(encode, aligned)
    pooled_maps = pooled_all.transpose(1, 0, 2, 3)
    inner_activation = residual(pooled_maps, inner_full, inner_bias, CUBE_PAD)
    narrowed_maps = reduce_resolution(inner_activation, narrowing_kernel, narrowing_bias)
    bottom_act = residual(narrowed_maps, bottom_full, bottom_bias, CUBE_PAD)
    lifted = upsample(bottom_act, lift_kernel, lift_bias, inner_activation)
    mended = residual(lifted, mend_kernel, mend_bias, PLANE_PAD)

    def decode(arrays):
        mended_plane, outer_plane = arrays
        expanded = upsample(mended_plane[:, None], expand_kernel, expand_bias, outer_plane[:, None])
        finished = residual(expanded, finish_kernel, finish_bias, PLANE_PAD)
        logits = jnp.einsum("oc,czyx->ozyx", head_kernel.astype(jnp.float32), finished.astype(jnp.float32), precision=HIGHEST)
        return jax.nn.sigmoid(logits + head_bias[:, None, None, None])[:, 0]

    affinity_all = lax.map(decode, (mended.transpose(1, 0, 2, 3), outer_all))
    return affinity_all.transpose(1, 0, 2, 3)
```

```python
import functools
import numpy as np
import jax
import jax.numpy as jnp
from jax import lax
from jax.experimental import pallas as pl
from jax.experimental.pallas import tpu as pltpu
from jax.sharding import PartitionSpec as P

BF = jnp.bfloat16
F32 = jnp.float32
PITCH = 40
NZ = 12
R12, R10, R8 = NZ * PITCH, 10 * PITCH, 8 * PITCH
PAD = 16


def stem_table():
    cols = [0, 1, 2, 3, 4, 5, -2, -1]
    outs = [(ro, j) for ro in range(2) for j in range(4)] + [(0, 4), (1, -1), (1, 4), (0, -1)]
    t = np.zeros((8, 4, 12, 3, 3), np.float32)
    for a, i in enumerate(cols):
        for r in range(4):
            for b, (ro, j) in enumerate(outs):
                dy, dx = r - ro, i - j + 1
                if 0 <= dy < 3 and 0 <= dx < 3:
                    t[a, r, b, dy, dx] = 1
    return t


def plane_table(width):
    ks = [(r, i) for r in range(4) for i in range(width)]
    if width == 4:
        for h in range(2):
            ks += [(2 * h, 4), (2 * h + 1, -1), (2 * h + 1, 4), (2 * h, -1)]
    else:
        for r in range(4):
            ks += [(r, 2), (r, -1)]
    outs = [(ro, j) for ro in range(2) for j in range(width)]
    t = np.zeros((len(ks), len(outs), 3, 3), np.float32)
    for a, (r, i) in enumerate(ks):
        for b, (ro, j) in enumerate(outs):
            dy, dx = r - ro, i - j + 1
            if 0 <= dy < 3 and 0 <= dx < 3:
                t[a, b, dy, dx] = 1
    return t


def prep_weights(w):
    d = {}
    base = jnp.einsum("arbyx,oyx->arbo", jnp.asarray(stem_table(), BF), w["stem_kernel"][:, 0, 0]).astype(BF)
    base = base.reshape(8, 4, 384)
    d["stem"] = jnp.stack([jnp.pad(base, ((0, 0), (2 * q, 28 - 2 * q), (0, 0))).reshape(256, 384) for q in range(15)])
    for name, width, ch in (("outer", 4, 32), ("finish", 4, 32), ("mend", 2, 64)):
        t = jnp.asarray(plane_table(width), BF)
        m = jnp.einsum("abyx,ocyx->acbo", t, w[name + "_kernel"][:, :, 0]).astype(BF)
        d[name] = m.reshape(t.shape[0] * ch, 256)
    t = jnp.asarray(plane_table(2), BF)
    kin = w["inner_kernel"].reshape(3, 3, 3, 64, 64)
    d["inner"] = jnp.einsum("abyx,zyxco->zacbo", t, kin).astype(BF).reshape(3, 1024, 256)
    kb = w["bottom_kernel"].reshape(3, 3, 3, 128, 128)
    rows = [[kb[:, r - ro] if 0 <= r - ro < 3 else jnp.zeros_like(kb[:, 0]) for ro in range(2)] for r in range(4)]
    d["bottom"] = jnp.stack([jnp.stack(q, 3) for q in rows], 1).reshape(3, 1536, 256)

    def down(k, width):
        eye = np.zeros((width, width // 2, 2), np.float32)
        for i in range(width):
            eye[i, i // 2, i % 2] = 1
        m = jnp.einsum("ijq,ocpq->picjo", jnp.asarray(eye, BF), k[:, :, 0]).astype(BF)
        return m.reshape(2 * width * k.shape[1], -1)

    def up(k, width):
        eye = np.zeros((width, width // 2, 2), np.float32)
        for i in range(width):
            eye[i, i // 2, i % 2] = 1
        m = jnp.einsum("ijq,copq->jcpio", jnp.asarray(eye, BF), k[:, :, 0]).astype(BF)
        return m.reshape(width // 2 * k.shape[0], -1)

    d["pool"] = down(w["pooling_kernel"], 4)
    d["narrow"] = down(w["narrowing_kernel"], 2)
    d["lift"] = up(w["lift_kernel"], 2)
    d["expand"] = up(w["expand_kernel"], 4)
    hk = w["head_kernel"]
    eye2 = jnp.eye(2, dtype=BF)
    h = jnp.einsum("rs,oc->roscj", eye2, hk)[:, :, :, None, :, 0] if False else None
    head = jnp.einsum("rs,j,oc->rosjc", eye2, jnp.ones((4,), BF), hk).astype(BF).reshape(6, 256)
    d["head"] = jnp.pad(head, ((0, 2), (0, 0)))
    b = {}
    s4 = jnp.tile(w["stem_bias"], 12)
    b["stem"] = s4[None]
    b["outer"] = jnp.tile(w["outer_bias"], 8)[None]
    b["finish"] = jnp.tile(w["finish_bias"], 8)[None]
    b["expand"] = jnp.tile(w["expand_bias"], 8)[None]
    b["pool"] = jnp.tile(w["pooling_bias"], 2)[None]
    b["inner"] = jnp.tile(w["inner_bias"], 4)[None]
    b["mend"] = jnp.tile(w["mend_bias"], 4)[None]
    b["lift"] = jnp.tile(w["lift_bias"], 4)[None]
    b["narrow"] = w["narrowing_bias"][None]
    b["bottom"] = jnp.tile(w["bottom_bias"], 2)[None]
    return d, b


WN = ("stem", "outer", "pool", "inner", "narrow", "bottom", "lift", "mend", "expand", "finish", "head")
BN = ("stem", "outer", "pool", "inner", "narrow", "bottom", "lift", "mend", "expand", "finish")


def dot(a, b):
    return jnp.dot(a, b, preferred_element_type=F32)


def compute(pos, counts, x4, W, B, out, sc):
    sec, gy, gx = pos
    nsec, ngy, ngx = counts
    lane = lax.broadcasted_iota(jnp.int32, (1, 128), 1)
    rows = lax.broadcasted_iota(jnp.int32, (R12, 1), 0)
    zi = rows // PITCH
    gi = rows - zi * PITCH
    zglob = sec * 8 - 2 + zi
    zok = jnp.logical_and(zglob >= 0, zglob < nsec * 8)
    gg = gx * 32 - 3 + gi

    def gok(shift):
        return jnp.logical_and(gg + shift >= 0, gg + shift < ngx * 32)

    m = jnp.broadcast_to(jnp.where(jnp.logical_and(zok, gok(0)), 1.0, 0.0), (R12, 128))
    sc.mask[0] = jnp.zeros((R12, 128), F32)
    sc.mask[1] = m
    sc.smask[0] = jnp.zeros((R12, 128), BF)
    sc.smask[1] = m.astype(BF)
    right = jnp.where(gok(1), 1.0, 0.0)
    left = jnp.where(gok(-1), 1.0, 0.0)
    zero = jnp.zeros((R12, 1), F32)
    for va in range(2):
        for vb in range(2):
            ra, la = (right, left) if va else (zero, zero)
            rb, lb = (right, left) if vb else (zero, zero)
            e = jnp.where(lane < 32, ra, jnp.where(lane < 64, lb, jnp.where(lane < 96, rb, la)))
            sc.emask[2 * va + vb] = e.astype(BF)

    def rowok(row, total):
        return jnp.where(jnp.logical_and(row >= 0, row < total), 1, 0)

    sc.xf[0:PAD] = jnp.zeros((PAD, 128), F32)
    sc.xf[PAD + R12 :] = jnp.zeros((PAD, 128), F32)
    for z in range(NZ):
        sc.xf[PAD + z * PITCH : PAD + (z + 1) * PITCH] = x4[z, 0:PITCH].astype(F32)
    sc.xin[:, 0:128] = sc.xf[PAD : PAD + R12].astype(BF)
    sc.xin[:, 128:256] = jnp.where(
        lane < 64, sc.xf[PAD + 1 : PAD + 1 + R12], sc.xf[PAD - 1 : PAD - 1 + R12]
    ).astype(BF)

    def stem(q, _):
        acc = dot(sc.xin[...], W["stem"][q]) + B["stem"][...]
        s = acc.astype(BF)
        va = rowok(gy * 8 + 2 * q - 11, ngy * 8)
        vb = rowok(gy * 8 + 2 * q - 10, ngy * 8)
        sc.s[2 * q] = s[:, 0:128]
        sc.s[2 * q + 1] = s[:, 128:256]
        r = jnp.maximum(s, jnp.zeros((), BF))
        sc.r[2 * q] = r[:, 0:128] * sc.smask[va]
        sc.r[2 * q + 1] = r[:, 128:256] * sc.smask[vb]
        sc.e[q] = r[:, 256:384] * sc.emask[2 * va + vb]
        return 0

    lax.fori_loop(0, 15, stem, 0)

    sc.pf[:, 0:PAD] = jnp.zeros((14, PAD, 128), F32)
    sc.pf[:, PAD + R12 :] = jnp.zeros((14, PAD, 128), F32)

    def outer(p, _):
        lhs = jnp.concatenate(
            [sc.r[2 * p], sc.r[2 * p + 1], sc.r[2 * p + 2], sc.r[2 * p + 3], sc.e[p], sc.e[p + 1]], axis=1
        )
        acc = dot(lhs, W["outer"][...])
        res = jnp.concatenate([sc.s[2 * p + 1], sc.s[2 * p + 2]], axis=1).astype(F32)
        o = (acc + res + B["outer"][...]).astype(BF)

        sc.o[p] = o[80:400]
        pooled = (dot(o, W["pool"][...]) + B["pool"][...]).astype(BF).astype(F32)
        v = rowok(gy * 4 + p - 5, ngy * 4)
        pooled = pooled * sc.mask[v]
        sc.pf[p, PAD : PAD + R12] = pooled
        sc.pa[p, :, 0:128] = jnp.maximum(pooled, 0.0).astype(BF)
        ea = jnp.where(lane < 64, sc.pf[p, PAD + 1 : PAD + 1 + R12], sc.pf[p, PAD - 1 : PAD - 1 + R12])
        sc.pa[p, :, 128:256] = jnp.maximum(ea, 0.0).astype(BF)
        sc.pb[p, :, 0:128] = jnp.maximum(sc.pf[p, PAD - 8 : PAD + 8 + R12], 0.0).astype(BF)
        eb = jnp.where(lane < 64, sc.pf[p, PAD - 7 : PAD + 9 + R12], sc.pf[p, PAD - 9 : PAD + 7 + R12])
        sc.pb[p, :, 128:256] = jnp.maximum(eb, 0.0).astype(BF)
        return 0

    lax.fori_loop(0, 14, outer, 0)

    sc.qf[:, 0:PAD] = jnp.zeros((6, PAD, 128), F32)
    sc.qf[:, PAD + R10 :] = jnp.zeros((6, PAD, 128), F32)

    def inner(k, _):
        acc = jnp.zeros((R10, 256), F32)
        for dz in range(3):
            src = (sc.pa, sc.pb, sc.pa)[dz]
            lo = (0, 48, 80)[dz]
            lhs = jnp.concatenate(
                [src[2 * k + r, lo : lo + R10, 0:128] for r in range(4)]
                + [src[2 * k + r, lo : lo + R10, 128:256] for r in range(4)],
                axis=1,
            )
            acc = acc + dot(lhs, W["inner"][dz])
        res = jnp.concatenate(
            [sc.pf[2 * k + 1, PAD + 40 : PAD + 440], sc.pf[2 * k + 2, PAD + 40 : PAD + 440]], axis=1
        )
        a = (acc + res + B["inner"][...]).astype(BF)
        sc.i[k] = a.astype(F32)[40:360].astype(BF)
        sq = (dot(a, W["narrow"][...]) + B["narrow"][...]).astype(BF).astype(F32)
        v = rowok(gy * 2 + k - 2, ngy * 2)
        sq = sq * sc.mask[v, 40:440]
        sc.qf[k, PAD : PAD + R10] = sq
        for d in range(3):
            sc.qa[k, :, d * 128 : (d + 1) * 128] = jnp.maximum(
                sc.qf[k, PAD - 1 + d : PAD - 1 + d + R10], 0.0
            ).astype(BF)
            sc.qb[k, :, d * 128 : (d + 1) * 128] = jnp.maximum(
                sc.qf[k, PAD - 9 + d : PAD + 7 + d + R10], 0.0
            ).astype(BF)
        return 0

    lax.fori_loop(0, 6, inner, 0)

    sc.lf[:, 0:PAD] = jnp.zeros((8, PAD, 128), F32)
    sc.lf[:, PAD + R8 :] = jnp.zeros((8, PAD, 128), F32)

    def bottom(mi, _):
        acc = jnp.zeros((R8, 256), F32)
        for dz in range(3):
            src = (sc.qa, sc.qb, sc.qa)[dz]
            lo = (0, 48, 80)[dz]
            lhs = jnp.concatenate([src[2 * mi + r, lo : lo + R8, :] for r in range(4)], axis=1)
            acc = acc + dot(lhs, W["bottom"][dz])
        res = jnp.concatenate(
            [sc.qf[2 * mi + 1, PAD + 40 : PAD + 360], sc.qf[2 * mi + 2, PAD + 40 : PAD + 360]], axis=1
        )
        a = (acc + res + B["bottom"][...]).astype(BF)
        for h in range(2):
            up = dot(a[:, h * 128 : (h + 1) * 128], W["lift"][...])
            y = 2 * mi + h
            l = (up + sc.i[y + 1].astype(F32) + B["lift"][...]).astype(BF).astype(F32)
            for e in range(2):
                t = 2 * y + e
                v = rowok(gy * 4 + t - 2, ngy * 4)
                lm = l[:, e * 128 : (e + 1) * 128] * sc.mask[v, 80:400]
                sc.lf[t, PAD : PAD + R8] = lm
                sc.la[t, :, 0:128] = jnp.maximum(lm, 0.0).astype(BF)
                ed = jnp.where(lane < 64, sc.lf[t, PAD + 1 : PAD + 1 + R8], sc.lf[t, PAD - 1 : PAD - 1 + R8])
                sc.la[t, :, 128:256] = jnp.maximum(ed, 0.0).astype(BF)
        return 0

    lax.fori_loop(0, 2, bottom, 0)

    sc.ef[:, 0:PAD] = jnp.zeros((12, PAD, 128), F32)
    sc.ef[:, PAD + R8 :] = jnp.zeros((12, PAD, 128), F32)

    def mend(n, _):
        lhs = jnp.concatenate(
            [sc.la[2 * n + r, :, 0:128] for r in range(4)] + [sc.la[2 * n + r, :, 128:256] for r in range(4)],
            axis=1,
        )
        acc = dot(lhs, W["mend"][...])
        res = jnp.concatenate(
            [sc.lf[2 * n + 1, PAD : PAD + R8], sc.lf[2 * n + 2, PAD : PAD + R8]], axis=1
        )
        a = (acc + res + B["mend"][...]).astype(BF)
        for h in range(2):
            j = 2 * n + h
            up = dot(a[:, h * 128 : (h + 1) * 128], W["expand"][...])
            x = (up + sc.o[4 + j].astype(F32) + B["expand"][...]).astype(BF).astype(F32)
            for e in range(2):
                t = 2 * j + e
                v = rowok(gy * 8 + t - 2, ngy * 8)
                xm = x[:, e * 128 : (e + 1) * 128] * sc.mask[v, 80:400]
                sc.ef[t, PAD : PAD + R8] = xm
                sc.ea[t] = jnp.maximum(xm, 0.0).astype(BF)
        return 0

    lax.fori_loop(0, 3, mend, 0)

    def edges(u, _):
        ta, tb = 2 * u + 1, 2 * u + 2
        ua = jnp.where(lane < 64, sc.ef[ta, PAD + 1 : PAD + 1 + R8], sc.ef[ta, PAD - 1 : PAD - 1 + R8])
        ub = jnp.where(lane < 64, sc.ef[tb, PAD + 1 : PAD + 1 + R8], sc.ef[tb, PAD - 1 : PAD - 1 + R8])
        ub = pltpu.roll(ub, 64, 1)
        e = jnp.where(jnp.logical_and(lane >= 32, lane < 96), ub, ua)
        sc.ee[u] = jnp.maximum(e, 0.0).astype(BF)
        return 0

    lax.fori_loop(0, 5, edges, 0)

    lane2 = lax.broadcasted_iota(jnp.int32, (1, 256), 1)
    jl = (lane2 // 32) % 4

    def finish(u, _):
        lhs = jnp.concatenate(
            [sc.ea[2 * u + 1 + r] for r in range(4)] + [sc.ee[u], sc.ee[u + 1]], axis=1
        )
        acc = dot(lhs, W["finish"][...])
        res = jnp.concatenate(
            [sc.ef[2 * u + 2, PAD : PAD + R8], sc.ef[2 * u + 3, PAD : PAD + R8]], axis=1
        )
        f = (acc + res + B["finish"][...]).astype(BF).astype(F32)
        sc.f[0:R8, 0] = f[:, 0:128]
        sc.f[0:R8, 1] = f[:, 128:256]
        return 0

    def finish2(u, _):
        lhs = jnp.concatenate(
            [sc.ea[2 * u + 1 + r] for r in range(4)] + [sc.ee[u], sc.ee[u + 1]], axis=1
        )
        acc = dot(lhs, W["finish"][...])
        res = jnp.concatenate(
            [sc.ef[2 * u + 2, PAD : PAD + R8], sc.ef[2 * u + 3, PAD : PAD + R8]], axis=1
        )
        f = (acc + res + B["finish"][...]).astype(BF).astype(F32)
        for h in range(2):
            sc.f[h, 0:R8] = f[:, h * 128 : (h + 1) * 128]
        for h in range(2):
            for z in range(8):
                fz = sc.f[h, z * PITCH + 3 : z * PITCH + 35]
                for j in range(4):
                    sc.g[h, pl.ds(z * 128 + j, 32, 4), :] = jnp.where(lane // 32 == j, fz, 0.0)
        for z in range(8):
            gz = jnp.concatenate([sc.g[h, z * 128 : (z + 1) * 128] for h in range(2)], axis=1).astype(BF)
            lt = lax.dot_general(W["head"][...], gz, (((1,), (1,)), ((), ())), preferred_element_type=F32)
            for ro in range(2):
                for o in range(3):
                    out[o, z, pl.ds(2 * u + ro, 1), :] = lt[ro * 3 + o : ro * 3 + o + 1]
        return 0

    lax.fori_loop(0, 4, finish2, 0)


SCRATCH = dict(
    mask=((2, R12, 128), F32),
    smask=((2, R12, 128), BF),
    emask=((4, R12, 128), BF),
    xf=((R12 + 2 * PAD, 128), F32),
    xin=((R12, 256), BF),
    s=((30, R12, 128), BF),
    r=((30, R12, 128), BF),
    e=((15, R12, 128), BF),
    o=((14, R8, 256), BF),
    pf=((14, R12 + 2 * PAD, 128), F32),
    pa=((14, R12, 256), BF),
    pb=((14, R12 + 16, 256), BF),
    i=((6, R8, 256), BF),
    qf=((6, R10 + 2 * PAD, 128), F32),
    qa=((6, R10, 384), BF),
    qb=((6, R10 + 16, 384), BF),
    lf=((8, R8 + 2 * PAD, 128), F32),
    la=((8, R8, 256), BF),
    ef=((12, R8 + 2 * PAD, 128), F32),
    ea=((12, R8, 128), BF),
    ee=((5, R8, 128), BF),
    f=((2, R8, 128), F32),
    g=((2, 1024, 128), F32),
)


class Refs:
    def __init__(self, names, refs):
        for n, r in zip(names, refs):
            setattr(self, n, r)


def unet_call(pos_fn, counts, x4, d, b, interpret=False):
    def body(*refs):
        x4r = refs[0]
        n = 1
        W = dict(zip(WN, refs[n : n + len(WN)]))
        n += len(WN)
        B = dict(zip(BN, refs[n : n + len(BN)]))
        n += len(BN)
        out = refs[n]
        sc = Refs(SCRATCH, refs[n + 1 :])
        compute(pos_fn(), counts, x4r, W, B, out, sc)

    vm = pl.BlockSpec(memory_space=pltpu.VMEM)
    return pl.pallas_call(
        body,
        out_shape=jax.ShapeDtypeStruct((3, 8, 8, 128), F32),
        in_specs=[vm] * (1 + len(WN) + len(BN)),
        out_specs=vm,
        scratch_shapes=[pltpu.VMEM(s, t) for s, t in SCRATCH.values()],
        compiler_params=pltpu.CompilerParams(vmem_limit_bytes=60 * 1024 * 1024),
        interpret=interpret,
    )(x4, *[d[k] for k in WN], *[b[k] for k in BN])
MESH = pl.DeviceIdType.MESH


def axis_position():
    return lax.axis_index("sec"), lax.axis_index("gy"), lax.axis_index("gx")


def align(own, left, right, off, has_left, has_right, cs):
    lane = lax.broadcasted_iota(jnp.int32, (1, 128), 1)

    def shifts(ref, first, ok):
        v = ref[64:80].astype(F32)
        m = jnp.concatenate([jnp.broadcast_to(v[first + i : first + i + 1], (8, 128)) for i in range(8)], axis=0)
        return m if ok is None else jnp.where(ok, m, -1.0)

    pix = [r[0:64].astype(F32) for r in (left, own, right)]
    oy = [shifts(left, 0, has_left), shifts(own, 0, None), shifts(right, 0, has_right)]
    ox = [shifts(left, 8, has_left), shifts(own, 8, None), shifts(right, 8, has_right)]
    rp = [pltpu.roll(p, 16, 1) for p in pix]
    for tile in range(2):
        raw = jnp.where(lane < 16, rp[tile], rp[tile + 1])
        oyt = jnp.where(lane < 16, oy[tile], oy[tile + 1])
        oxt = jnp.where(lane < 16, ox[tile], ox[tile + 1])
        for s in range(5):
            hit = oxt == float(s)
            v = jnp.where(hit, raw, 0.0)
            o = jnp.where(hit, oyt, -1.0)
            cs.vs[s, tile] = v if s == 0 else pltpu.roll(v, s, 1)
            cs.os[s, tile] = o if s == 0 else pltpu.roll(o, s, 1)
    cs.vb[:, :, 0:8] = jnp.zeros((2, 2, 8, 128), F32)
    for tile in range(2):
        total = jnp.zeros((64, 128), F32)
        cover = jnp.zeros((64, 128), F32)
        for t in range(5):
            v = jnp.zeros((64, 128), F32)
            c = jnp.zeros((64, 128), F32)
            for s in range(5):
                vs, os = cs.vs[s, tile], cs.os[s, tile]
                if tile == 1 and s > 0:
                    vs = jnp.where(lane < s, cs.vs[s, 0], vs)
                    os = jnp.where(lane < s, cs.os[s, 0], os)
                hit = os == float(t)
                v = v + jnp.where(hit, vs, 0.0)
                c = c + jnp.where(hit, 1.0, 0.0)
            if t > 0:
                cs.vb[tile, 0, 8:72] = v
                cs.vb[tile, 1, 8:72] = c
                v = cs.vb[tile, 0, 8 - t : 72 - t]
                c = cs.vb[tile, 1, 8 - t : 72 - t]
            total = total + v
            cover = cover + c
        a = (total / jnp.maximum(cover, 1.0)).astype(BF).astype(F32)
        if tile == 0:
            a = jnp.where(jnp.logical_or(lane >= 16, has_left), a, 0.0)
        else:
            a = jnp.where(jnp.logical_or(lane < 16, has_right), a, 0.0)
        a = jnp.concatenate([a, jnp.zeros((64, 128), F32)], axis=0)
        cs.tt[tile * 128 : (tile + 1) * 128] = a.T
    xs = [cs.tt[pl.ds(4 + i, 48, 4), :] for i in range(4)]
    for g in range(8):
        piece = jnp.zeros((48, 128), F32)
        for i in range(4):
            sh = (32 * i - (8 * g - 12)) % 128
            r = xs[i] if sh == 0 else pltpu.roll(xs[i], sh, 1)
            piece = jnp.where(lane // 32 == i, r, piece)
        cs.sbuf[g] = piece.astype(BF)


CS = dict(
    near=((80, 128), BF),
    rb=((2, 80, 128), BF),
    sbuf=((8, 48, 128), BF),
    rx=((NZ, 48, 128), BF),
    vs=((5, 2, 64, 128), F32),
    os=((5, 2, 64, 128), F32),
    vb=((2, 2, 72, 128), F32),
    tt=((256, 128), F32),
)


def gather(img, off, cs, sems, counts):
    send1, recv1, send2, send3, recv2 = sems
    sec, gy, gx = axis_position()
    nsec, ngy, ngx = counts
    one = jnp.int32(1)
    has_left, has_right = gx > 0, gx < ngx - 1
    above, below = sec > 0, sec < nsec - 1
    barrier = pltpu.get_barrier_semaphore()

    def greet(*device):
        pl.semaphore_signal(barrier, inc=1, device_id=device, device_id_type=MESH)

    cs.rx[...] = jnp.zeros((NZ, 48, 128), BF)
    cs.rb[...] = jnp.zeros((2, 80, 128), BF)

    @pl.when(has_left)
    def _():
        greet(sec, gy, gx - 1)

    @pl.when(has_right)
    def _():
        greet(sec, gy, gx + 1)

    for k in range(1, 8):
        greet(sec, lax.rem(gy + k, 8), gx)

    @pl.when(below)
    def _():
        greet(sec + 1, 0 * gy, gx)
        greet(sec + 1, 0 * gy + 1, gx)

    @pl.when(above)
    def _():
        greet(sec - 1, 0 * gy + 6, gx)
        greet(sec - 1, 0 * gy + 7, gx)

    to_up = jnp.logical_and(gy < 2, above)
    to_down = jnp.logical_and(gy >= 6, below)
    expect = 7 + jnp.where(has_left, 1, 0) + jnp.where(has_right, 1, 0) + jnp.where(jnp.logical_or(to_up, to_down), 8, 0)

    cs.near[0:64] = img[...]
    r16 = lax.broadcasted_iota(jnp.int32, (16, 128), 0)
    info = jnp.zeros((16, 128), F32)
    for i in range(8):
        info = jnp.where(r16 == i, off[i, 0].astype(F32), info)
        info = jnp.where(r16 == 8 + i, off[i, 1].astype(F32), info)
    cs.near[64:80] = info.astype(BF)

    pl.semaphore_wait(barrier, expect)

    def near_copy(slot, target):
        return pltpu.make_async_remote_copy(
            src_ref=cs.near, dst_ref=cs.rb.at[slot], send_sem=send1.at[slot], recv_sem=recv1.at[slot],
            device_id=(sec, gy, target), device_id_type=MESH,
        )

    @pl.when(has_right)
    def _():
        near_copy(0, gx + 1).start()

    @pl.when(has_left)
    def _():
        near_copy(1, gx - 1).start()

    @pl.when(has_left)
    def _():
        near_copy(0, gx - 1).wait_recv()

    @pl.when(has_right)
    def _():
        near_copy(1, gx + 1).wait_recv()

    align(cs.near, cs.rb.at[0], cs.rb.at[1], off, has_left, has_right, cs)

    def far(g, slot, s, sem):
        return pltpu.make_async_remote_copy(
            src_ref=cs.sbuf.at[g], dst_ref=cs.rx.at[slot], send_sem=sem.at[g], recv_sem=recv2.at[slot],
            device_id=(s, g, gx), device_id_type=MESH,
        )

    for k in range(1, 8):
        far(lax.rem(gy + k, 8), gy + 2, sec, send2).start()

    @pl.when(to_up)
    def _():
        for k in range(8):
            far(lax.rem(gy + k, 8), gy + 10, sec - 1, send3).start()

    @pl.when(to_down)
    def _():
        for k in range(8):
            far(lax.rem(gy + k, 8), gy - 6, sec + 1, send3).start()

    cs.rx[gy + 2] = cs.sbuf[gy]

    def finish():
        for k in range(1, 8):
            far(lax.rem(gy + k, 8), 2 + lax.rem(gy + k, 8), sec, send2).wait_recv()

        @pl.when(above)
        def _():
            for slot in (0, 1):
                far(lax.rem(gy + 1, 8), slot, sec - 1, send3).wait_recv()

        @pl.when(below)
        def _():
            for slot in (10, 11):
                far(lax.rem(gy + 1, 8), slot, sec + 1, send3).wait_recv()

    def drain():
        @pl.when(has_right)
        def _():
            near_copy(0, gx + 1).wait_send()

        @pl.when(has_left)
        def _():
            near_copy(1, gx - 1).wait_send()

        for k in range(1, 8):
            far(lax.rem(gy + k, 8), gy + 2, sec, send2).wait_send()

        @pl.when(to_up)
        def _():
            for k in range(8):
                far(lax.rem(gy + k, 8), gy + 10, sec - 1, send3).wait_send()

        @pl.when(to_down)
        def _():
            for k in range(8):
                far(lax.rem(gy + k, 8), gy - 6, sec + 1, send3).wait_send()

    return finish, drain


def gather_call(images, offsets, counts):
    def body(img, off, out, *rest):
        cs = Refs(CS, rest[: len(CS)])
        finish, drain = gather(img, off, cs, rest[len(CS) :], counts)
        finish()
        drain()
        out[...] = cs.rx[...]

    dma = pltpu.SemaphoreType.DMA
    return pl.pallas_call(
        body,
        out_shape=jax.ShapeDtypeStruct((NZ, 48, 128), BF),
        in_specs=[pl.BlockSpec(memory_space=pltpu.VMEM), pl.BlockSpec(memory_space=pltpu.SMEM)],
        out_specs=pl.BlockSpec(memory_space=pltpu.VMEM),
        scratch_shapes=[pltpu.VMEM(s, t) for s, t in CS.values()]
        + [dma((2,)), dma((2,)), dma((8,)), dma((8,)), dma((12,))],
        compiler_params=pltpu.CompilerParams(
            vmem_limit_bytes=24 * 1024 * 1024, collective_id=0, has_side_effects=True
        ),
    )(images, offsets)


NAMES = (
    "images", "offsets", "stem_kernel", "stem_bias", "outer_kernel", "outer_bias", "pooling_kernel",
    "pooling_bias", "inner_kernel", "inner_bias", "narrowing_kernel", "narrowing_bias", "bottom_kernel",
    "bottom_bias", "lift_kernel", "lift_bias", "mend_kernel", "mend_bias", "expand_kernel", "expand_bias",
    "finish_kernel", "finish_bias", "head_kernel", "head_bias",
)


def solution(mesh):
    counts = (mesh.shape["sec"], mesh.shape["gy"], mesh.shape["gx"])

    def per_device(*args):
        w = dict(zip(NAMES, args))
        x4 = gather_call(w["images"].reshape(64, 128), w["offsets"].reshape(8, 2), counts)
        d, b = prep_weights(w)
        logits = unet_call(axis_position, counts, x4, d, b)
        return jax.nn.sigmoid(logits + w["head_bias"][:, None, None, None])

    in_specs = (P(("sec", "gy"), None, "gx"), P(("sec", "gy"), None, None, "gx")) + (P(),) * 22
    out_specs = P(None, "sec", "gy", "gx")
    return jax.shard_map(per_device, mesh=mesh, in_specs=in_specs, out_specs=out_specs, check_vma=False)
```

```python
import jax
import jax.numpy as jnp
from jax import lax
from jax.experimental import pallas as pl
from jax.experimental.pallas import tpu as pltpu
from jax.sharding import PartitionSpec as P

BF = jnp.bfloat16
F32 = jnp.float32
PITCH = 40
NZ = 12
R12, R10, R8 = NZ * PITCH, 10 * PITCH, 8 * PITCH
PAD = 16


WN = ("stem", "outer", "pool", "inner", "narrow", "bottom", "lift", "mend", "expand", "finish", "head")
BN = ("stem", "outer", "pool", "inner", "narrow", "bottom", "lift", "mend", "expand", "finish")


def dot(a, b):
    return jnp.dot(a, b, preferred_element_type=F32)


def compute(pos, counts, x4, W, B, out, sc):
    sec, gy, gx = pos
    nsec, ngy, ngx = counts
    lane = lax.broadcasted_iota(jnp.int32, (1, 128), 1)
    rows = lax.broadcasted_iota(jnp.int32, (R12, 1), 0)
    zi = rows // PITCH
    gi = rows - zi * PITCH
    zglob = sec * 8 - 2 + zi
    zok = jnp.logical_and(zglob >= 0, zglob < nsec * 8)
    gg = gx * 32 - 3 + gi

    def gok(shift):
        return jnp.logical_and(gg + shift >= 0, gg + shift < ngx * 32)

    m = jnp.broadcast_to(jnp.where(jnp.logical_and(zok, gok(0)), 1.0, 0.0), (R12, 128))
    sc.mask[0] = jnp.zeros((R12, 128), F32)
    sc.mask[1] = m
    sc.smask[0] = jnp.zeros((R12, 128), BF)
    sc.smask[1] = m.astype(BF)
    right = jnp.where(gok(1), 1.0, 0.0)
    left = jnp.where(gok(-1), 1.0, 0.0)
    zero = jnp.zeros((R12, 1), F32)
    for va in range(2):
        for vb in range(2):
            ra, la = (right, left) if va else (zero, zero)
            rb, lb = (right, left) if vb else (zero, zero)
            e = jnp.where(lane < 32, ra, jnp.where(lane < 64, lb, jnp.where(lane < 96, rb, la)))
            sc.emask[2 * va + vb] = e.astype(BF)

    def rowok(row, total):
        return jnp.where(jnp.logical_and(row >= 0, row < total), 1, 0)

    sc.xf[0:PAD] = jnp.zeros((PAD, 128), F32)
    sc.xf[PAD + R12 :] = jnp.zeros((PAD, 128), F32)
    for z in range(NZ):
        sc.xf[PAD + z * PITCH : PAD + (z + 1) * PITCH] = x4[z, 0:PITCH].astype(F32)
    sc.xin[:, 0:128] = sc.xf[PAD : PAD + R12].astype(BF)
    sc.xin[:, 128:256] = jnp.where(
        lane < 64, sc.xf[PAD + 1 : PAD + 1 + R12], sc.xf[PAD - 1 : PAD - 1 + R12]
    ).astype(BF)

    def stem(q, _):
        acc = dot(sc.xin[...], W["stem"][q]) + B["stem"][...]
        s = acc.astype(BF)
        va = rowok(gy * 8 + 2 * q - 11, ngy * 8)
        vb = rowok(gy * 8 + 2 * q - 10, ngy * 8)
        sc.s[2 * q] = s[:, 0:128]
        sc.s[2 * q + 1] = s[:, 128:256]
        r = jnp.maximum(s, jnp.zeros((), BF))
        sc.r[2 * q] = r[:, 0:128] * sc.smask[va]
        sc.r[2 * q + 1] = r[:, 128:256] * sc.smask[vb]
        sc.e[q] = r[:, 256:384] * sc.emask[2 * va + vb]
        return 0

    lax.fori_loop(0, 15, stem, 0)

    sc.pf[:, 0:PAD] = jnp.zeros((14, PAD, 128), F32)
    sc.pf[:, PAD + R12 :] = jnp.zeros((14, PAD, 128), F32)

    def outer(p, _):
        lhs = jnp.concatenate(
            [sc.r[2 * p], sc.r[2 * p + 1], sc.r[2 * p + 2], sc.r[2 * p + 3], sc.e[p], sc.e[p + 1]], axis=1
        )
        acc = dot(lhs, W["outer"][...])
        res = jnp.concatenate([sc.s[2 * p + 1], sc.s[2 * p + 2]], axis=1).astype(F32)
        o = (acc + res + B["outer"][...]).astype(BF)

        @pl.when(jnp.logical_and(p >= 4, p < 10))
        def _():
            sc.o[p - 4] = o[80:400]

        pooled = (dot(o, W["pool"][...]) + B["pool"][...]).astype(BF).astype(F32)
        v = rowok(gy * 4 + p - 5, ngy * 4)
        pooled = pooled * sc.mask[v]
        sc.pf[p, PAD : PAD + R12] = pooled
        sc.pa[p, :, 0:128] = jnp.maximum(pooled, 0.0).astype(BF)
        ea = jnp.where(lane < 64, sc.pf[p, PAD + 1 : PAD + 1 + R12], sc.pf[p, PAD - 1 : PAD - 1 + R12])
        sc.pa[p, :, 128:256] = jnp.maximum(ea, 0.0).astype(BF)
        sc.pb[p, :, 0:128] = jnp.maximum(sc.pf[p, PAD - 8 : PAD + 8 + R12], 0.0).astype(BF)
        eb = jnp.where(lane < 64, sc.pf[p, PAD - 7 : PAD + 9 + R12], sc.pf[p, PAD - 9 : PAD + 7 + R12])
        sc.pb[p, :, 128:256] = jnp.maximum(eb, 0.0).astype(BF)
        return 0

    lax.fori_loop(0, 14, outer, 0)

    sc.qf[:, 0:PAD] = jnp.zeros((6, PAD, 128), F32)
    sc.qf[:, PAD + R10 :] = jnp.zeros((6, PAD, 128), F32)

    def inner(k, _):
        acc = jnp.zeros((R10, 256), F32)
        for dz in range(3):
            src = (sc.pa, sc.pb, sc.pa)[dz]
            lo = (0, 48, 80)[dz]
            lhs = jnp.concatenate(
                [src[2 * k + r, lo : lo + R10, 0:128] for r in range(4)]
                + [src[2 * k + r, lo : lo + R10, 128:256] for r in range(4)],
                axis=1,
            )
            acc = acc + dot(lhs, W["inner"][dz])
        res = jnp.concatenate(
            [sc.pf[2 * k + 1, PAD + 40 : PAD + 440], sc.pf[2 * k + 2, PAD + 40 : PAD + 440]], axis=1
        )
        a = (acc + res + B["inner"][...]).astype(BF)
        sc.i[k] = a.astype(F32)[40:360].astype(BF)
        sq = (dot(a, W["narrow"][...]) + B["narrow"][...]).astype(BF).astype(F32)
        v = rowok(gy * 2 + k - 2, ngy * 2)
        sq = sq * sc.mask[v, 40:440]
        sc.qf[k, PAD : PAD + R10] = sq
        for d in range(3):
            sc.qa[k, :, d * 128 : (d + 1) * 128] = jnp.maximum(
                sc.qf[k, PAD - 1 + d : PAD - 1 + d + R10], 0.0
            ).astype(BF)
            sc.qb[k, :, d * 128 : (d + 1) * 128] = jnp.maximum(
                sc.qf[k, PAD - 9 + d : PAD + 7 + d + R10], 0.0
            ).astype(BF)
        return 0

    lax.fori_loop(0, 6, inner, 0)

    sc.lf[:, 0:PAD] = jnp.zeros((8, PAD, 128), F32)
    sc.lf[:, PAD + R8 :] = jnp.zeros((8, PAD, 128), F32)

    def bottom(mi, _):
        acc = jnp.zeros((R8, 256), F32)
        for dz in range(3):
            src = (sc.qa, sc.qb, sc.qa)[dz]
            lo = (0, 48, 80)[dz]
            lhs = jnp.concatenate([src[2 * mi + r, lo : lo + R8, :] for r in range(4)], axis=1)
            acc = acc + dot(lhs, W["bottom"][dz])
        res = jnp.concatenate(
            [sc.qf[2 * mi + 1, PAD + 40 : PAD + 360], sc.qf[2 * mi + 2, PAD + 40 : PAD + 360]], axis=1
        )
        a = (acc + res + B["bottom"][...]).astype(BF)
        for h in range(2):
            up = dot(a[:, h * 128 : (h + 1) * 128], W["lift"][...])
            y = 2 * mi + h
            l = (up + sc.i[y + 1].astype(F32) + B["lift"][...]).astype(BF).astype(F32)
            for e in range(2):
                t = 2 * y + e
                v = rowok(gy * 4 + t - 2, ngy * 4)
                lm = l[:, e * 128 : (e + 1) * 128] * sc.mask[v, 80:400]
                sc.lf[t, PAD : PAD + R8] = lm
                sc.la[t, :, 0:128] = jnp.maximum(lm, 0.0).astype(BF)
                ed = jnp.where(lane < 64, sc.lf[t, PAD + 1 : PAD + 1 + R8], sc.lf[t, PAD - 1 : PAD - 1 + R8])
                sc.la[t, :, 128:256] = jnp.maximum(ed, 0.0).astype(BF)
        return 0

    lax.fori_loop(0, 2, bottom, 0)

    sc.ef[:, 0:PAD] = jnp.zeros((12, PAD, 128), F32)
    sc.ef[:, PAD + R8 :] = jnp.zeros((12, PAD, 128), F32)

    def mend(n, _):
        lhs = jnp.concatenate(
            [sc.la[2 * n + r, :, 0:128] for r in range(4)] + [sc.la[2 * n + r, :, 128:256] for r in range(4)],
            axis=1,
        )
        acc = dot(lhs, W["mend"][...])
        res = jnp.concatenate(
            [sc.lf[2 * n + 1, PAD : PAD + R8], sc.lf[2 * n + 2, PAD : PAD + R8]], axis=1
        )
        a = (acc + res + B["mend"][...]).astype(BF)
        for h in range(2):
            j = 2 * n + h
            up = dot(a[:, h * 128 : (h + 1) * 128], W["expand"][...])
            x = (up + sc.o[j].astype(F32) + B["expand"][...]).astype(BF).astype(F32)
            for e in range(2):
                t = 2 * j + e
                v = rowok(gy * 8 + t - 2, ngy * 8)
                xm = x[:, e * 128 : (e + 1) * 128] * sc.mask[v, 80:400]
                sc.ef[t, PAD : PAD + R8] = xm
                sc.ea[t] = jnp.maximum(xm, 0.0).astype(BF)
        return 0

    lax.fori_loop(0, 3, mend, 0)

    def edges(u, _):
        ta, tb = 2 * u + 1, 2 * u + 2
        ua = jnp.where(lane < 64, sc.ef[ta, PAD + 1 : PAD + 1 + R8], sc.ef[ta, PAD - 1 : PAD - 1 + R8])
        ub = jnp.where(lane < 64, sc.ef[tb, PAD + 1 : PAD + 1 + R8], sc.ef[tb, PAD - 1 : PAD - 1 + R8])
        ub = pltpu.roll(ub, 64, 1)
        e = jnp.where(jnp.logical_and(lane >= 32, lane < 96), ub, ua)
        sc.ee[u] = jnp.maximum(e, 0.0).astype(BF)
        return 0

    lax.fori_loop(0, 5, edges, 0)

    lane2 = lax.broadcasted_iota(jnp.int32, (1, 256), 1)
    jl = (lane2 // 32) % 4

    def finish(u, _):
        lhs = jnp.concatenate(
            [sc.ea[2 * u + 1 + r] for r in range(4)] + [sc.ee[u], sc.ee[u + 1]], axis=1
        )
        acc = dot(lhs, W["finish"][...])
        res = jnp.concatenate(
            [sc.ef[2 * u + 2, PAD : PAD + R8], sc.ef[2 * u + 3, PAD : PAD + R8]], axis=1
        )
        f = (acc + res + B["finish"][...]).astype(BF).astype(F32)
        for h in range(2):
            sc.f[h, 0:R8] = f[:, h * 128 : (h + 1) * 128]
        for h in range(2):
            for z in range(8):
                fz = sc.f[h, z * PITCH + 3 : z * PITCH + 35]
                for j in range(4):
                    sc.g[h, pl.ds(z * 128 + j, 32, 4), :] = jnp.where(lane // 32 == j, fz, 0.0)
        for z in range(8):
            gz = jnp.concatenate([sc.g[h, z * 128 : (z + 1) * 128] for h in range(2)], axis=1).astype(BF)
            lt = lax.dot_general(W["head"][...], gz, (((1,), (1,)), ((), ())), preferred_element_type=F32)
            for ro in range(2):
                for o in range(3):
                    out[o, z, pl.ds(2 * u + ro, 1), :] = lt[ro * 3 + o : ro * 3 + o + 1]
        return 0

    lax.fori_loop(0, 4, finish, 0)


SCRATCH = dict(
    mask=((2, R12, 128), F32),
    smask=((2, R12, 128), BF),
    emask=((4, R12, 128), BF),
    xf=((R12 + 2 * PAD, 128), F32),
    xin=((R12, 256), BF),
    s=((30, R12, 128), BF),
    r=((30, R12, 128), BF),
    e=((15, R12, 128), BF),
    o=((6, R8, 256), BF),
    pf=((14, R12 + 2 * PAD, 128), F32),
    pa=((14, R12, 256), BF),
    pb=((14, R12 + 16, 256), BF),
    i=((6, R8, 256), BF),
    qf=((6, R10 + 2 * PAD, 128), F32),
    qa=((6, R10, 384), BF),
    qb=((6, R10 + 16, 384), BF),
    lf=((8, R8 + 2 * PAD, 128), F32),
    la=((8, R8, 256), BF),
    ef=((12, R8 + 2 * PAD, 128), F32),
    ea=((12, R8, 128), BF),
    ee=((5, R8, 128), BF),
    f=((2, R8, 128), F32),
    g=((2, 1024, 128), F32),
)


class Refs:
    def __init__(self, names, refs):
        for n, r in zip(names, refs):
            setattr(self, n, r)


WS = dict(
    stem=((15, 256, 384), BF),
    outer=((768, 256), BF),
    pool=((256, 128), BF),
    inner=((3, 1024, 256), BF),
    narrow=((256, 128), BF),
    bottom=((3, 1536, 256), BF),
    lift=((128, 256), BF),
    mend=((1024, 256), BF),
    expand=((128, 256), BF),
    finish=((768, 256), BF),
    head=((8, 256), BF),
)
BS = dict(
    stem=(1, 384), outer=(1, 256), pool=(1, 128), inner=(1, 256), narrow=(1, 128), bottom=(1, 256),
    lift=(1, 256), mend=(1, 256), expand=(1, 256), finish=(1, 256),
)
RAW = dict(
    stem=(3, 3, 32), outer=(3, 3, 32, 32), pool=(32, 2, 2, 64), inner=(3, 3, 3, 4096), narrow=(64, 2, 2, 128),
    bottom=(3, 3, 3, 16384), lift=(64, 2, 2, 128), mend=(3, 3, 64, 64), expand=(32, 2, 2, 64),
    finish=(3, 3, 32, 32), head=(3, 32),
)
RAWB = dict(stem=32, outer=32, pool=64, inner=64, narrow=128, bottom=128, lift=64, mend=64, expand=32, finish=32)
LONG = dict(
    stem="stem", outer="outer", pool="pooling", inner="inner", narrow="narrowing", bottom="bottom", lift="lift",
    mend="mend", expand="expand", finish="finish",
)
PS = dict(
    st=((128 * 8, 128), F32),
    sw=((288, 384), F32),
    tb=((27, 128, 128), BF),
)


def raw_views(w):
    def plane(k):
        return k[:, :, 0].transpose(2, 3, 0, 1)

    def inward(k):
        return k[:, :, 0].transpose(1, 2, 3, 0)

    raw = dict(
        stem=w["stem_kernel"][:, 0, 0].transpose(1, 2, 0),
        outer=plane(w["outer_kernel"]), mend=plane(w["mend_kernel"]), finish=plane(w["finish_kernel"]),
        pool=inward(w["pooling_kernel"]), narrow=inward(w["narrowing_kernel"]),
        lift=inward(w["lift_kernel"]), expand=inward(w["expand_kernel"]),
        inner=w["inner_kernel"], bottom=w["bottom_kernel"], head=w["head_kernel"],
    )
    bias = {k: w[LONG[k] + "_bias"].reshape(1, -1) for k in RAWB}
    return raw, bias


def iota(shape, dim):
    return lax.broadcasted_iota(jnp.int32, shape, dim)


def onehot(cond):
    return jnp.where(cond, 1.0, 0.0).astype(BF)


def prep_bias(raw, B):
    for k, n in RAWB.items():
        v = raw[k][...]
        reps = BS[k][1] // n
        B[k][...] = v if reps == 1 else jnp.concatenate([v] * reps, axis=1)


def prep_stem(raw, W, ps):
    k = jnp.concatenate([raw["stem"][dy].astype(F32) for dy in range(3)] + [jnp.zeros((7, 32), F32)], axis=0)
    e = onehot(iota((32, 384), 0) == iota((32, 384), 1) % 32)
    kt = dot(k.astype(BF), e)
    row, lane = iota((32, 384), 0), iota((32, 384), 1)
    a, r, slot = row // 4, row % 4, lane // 32
    i = jnp.where(a < 6, a, a - 8)
    edge = slot >= 8
    ro = jnp.where(edge, jnp.where(jnp.logical_or(slot == 8, slot == 11), 0, 1), slot // 4)
    j = jnp.where(edge, jnp.where(slot % 2 == 0, 4, -1), slot % 4)
    dy, dx = r - ro, i - j + 1
    ok = jnp.logical_and(jnp.logical_and(dy >= 0, dy < 3), jnp.logical_and(dx >= 0, dx < 3))
    idx = jnp.where(ok, 3 * dy + dx, -1)
    base = jnp.zeros((32, 384), F32)
    for d in range(9):
        base = jnp.where(idx == d, kt[d : d + 1], base)
    ps.sw[...] = jnp.zeros((288, 384), F32)
    for a in range(8):
        ps.sw[32 + a * 32 : 36 + a * 32] = base[4 * a : 4 * a + 4]
    for q in range(15):
        W["stem"][q] = ps.sw[32 - 2 * q : 288 - 2 * q].astype(BF)


def prep_plane(k, W, ch, ps):

    flat = jnp.concatenate([k[dy, dx] for dy in range(3) for dx in range(3)], axis=0)
    e = onehot(iota((128, ch), 0) % ch == iota((128, ch), 1))
    t = lax.dot_general(e, flat, (((1,), (1,)), ((), ())), preferred_element_type=F32).astype(BF)
    n = 9 * ch
    er, el = iota((n, 1152), 0), iota((n, 1152), 1)
    spread = onehot(jnp.logical_and(er // ch == el // 128, er % ch == el % ch))
    t = dot(t, spread).astype(BF)
    blocks = [[t[:, (3 * dy + dx) * 128 : (3 * dy + dx + 1) * 128] for dx in range(3)] for dy in range(3)]
    place_plane(blocks, W, ch)


def place_plane(blocks, W, ch, base=None):
    width = 128 // ch
    row, lane = iota((128, 128), 0), iota((128, 128), 1)
    i, j = row // ch, lane // ch
    zero = jnp.zeros((128, 128), F32)
    b32 = [[b.astype(F32) for b in q] for q in blocks]
    diag = []
    for dy in range(3):
        m = zero
        for dx in range(3):
            m = jnp.where(i - j + 1 == dx, b32[dy][dx], m)
        diag.append(m.astype(BF))
    zb = zero.astype(BF)

    def put(at, ro, v):
        if base is None:
            W[at : at + 128, ro * 128 : (ro + 1) * 128] = v
        else:
            W[base, at : at + 128, ro * 128 : (ro + 1) * 128] = v

    for r in range(4):
        for ro in range(2):
            put(r * 128, ro, diag[r - ro] if 0 <= r - ro < 3 else zb)

    def side(dy, dx):
        if not 0 <= dy < 3:
            return zero
        return jnp.where(j == (width - 1 if dx == 2 else 0), b32[dy][dx], 0.0)

    if ch == 32:
        for h in range(2):
            for ro in range(2):
                a, b = 2 * h - ro, 2 * h + 1 - ro
                v = jnp.where(i == 0, side(a, 2), jnp.where(i == 1, side(b, 0), jnp.where(i == 2, side(b, 2), side(a, 0))))
                put(512 + h * 128, ro, v.astype(BF))
    else:
        for r in range(4):
            for ro in range(2):
                v = jnp.where(i == 0, side(r - ro, 2), side(r - ro, 0))
                put(512 + r * 128, ro, v.astype(BF))


def prep_inner(k, W, ps):
    s = onehot(
        jnp.logical_and(iota((128, 256), 0) // 64 == iota((128, 256), 1) // 128,
                        iota((128, 256), 0) % 64 == iota((128, 256), 1) % 64)
    )
    ra, rl = iota((128, 64), 0), iota((128, 64), 1)
    a = onehot((ra % 64) == 2 * (rl % 32) + rl // 32)

    def plane(zy, _):
        dz = zy // 3
        dy = zy - 3 * dz
        for p in range(32):
            ps.st[p * 8 : p * 8 + 3] = k[dz, dy, :, p * 128 : (p + 1) * 128].astype(F32)
        for dx in range(3):
            m = dot(ps.st[pl.ds(dx, 32, 8), :].astype(BF), s)
            m = jnp.concatenate([m[:, 0:128], m[:, 128:256]], axis=0).astype(BF)
            ps.tb[3 * zy + dx] = dot(a, m).astype(BF)
        return 0

    lax.fori_loop(0, 9, plane, 0)
    for dz in range(3):
        blocks = [[ps.tb[9 * dz + 3 * dy + dx] for dx in range(3)] for dy in range(3)]
        place_plane(blocks, W, 64, base=dz)


def prep_bottom(k, W, ps):
    zb = jnp.zeros((384, 128), BF)
    for dz in range(3):
        W[dz, 0:384, 128:256] = zb
        W[dz, 1152:1536, 0:128] = zb

    def plane(zy, _):
        dz = zy // 3
        dy = zy - 3 * dz
        for c in range(128):
            ps.st[c * 8 : c * 8 + 3] = k[dz, dy, :, c * 128 : (c + 1) * 128].astype(F32)
        for dx in range(3):
            m = ps.st[pl.ds(dx, 128, 8), :].astype(BF)
            W[dz, pl.ds(pl.multiple_of(dy * 384 + dx * 128, 128), 128), 0:128] = m
            W[dz, pl.ds(pl.multiple_of(dy * 384 + 384 + dx * 128, 128), 128), 128:256] = m
        return 0

    lax.fori_loop(0, 9, plane, 0)


def corners(k, ch, ps):
    n = k.shape[3]
    for c in range(ch):
        for p in range(2):
            v = k[c, p].astype(F32)
            ps.st[(2 * c + p) * 8 : (2 * c + p) * 8 + 2, 0:n] = v
    return [[ps.st[pl.ds(8 * p + q, ch, 16), :] for q in range(2)] for p in range(2)]


def prep_corners(raw, W, ps):
    lane = iota((32, 128), 1)
    for name in ("pool", "expand"):
        x = corners(raw[name], 32, ps)
        rows = []
        for p in range(2):
            for i in range(4):
                v = jnp.where(lane < 64, x[p][i % 2], 0.0)
                rows.append(v if i < 2 else pltpu.roll(v, 64, 1))
        z = jnp.concatenate(rows, axis=0)
        if name == "pool":
            W["pool"][...] = z.astype(BF)
        else:
            W["expand"][...] = jnp.concatenate([z[0:128].T, z[128:256].T], axis=1).astype(BF)
    x = corners(raw["narrow"], 64, ps)
    W["narrow"][...] = jnp.concatenate([x[p][q] for p in range(2) for q in range(2)], axis=0).astype(BF)
    x = corners(raw["lift"], 64, ps)
    z = [jnp.concatenate([x[p][0], x[p][1]], axis=0) for p in range(2)]
    W["lift"][...] = jnp.concatenate([z[0].T, z[1].T], axis=1).astype(BF)


def prep_head(raw, W):
    h = raw["head"][...].astype(F32)
    h = jnp.concatenate([h, h, jnp.zeros((2, 32), F32)], axis=0).astype(BF)
    e = onehot(iota((32, 256), 0) == iota((32, 256), 1) % 32)
    t = dot(h, e)
    row, lane = iota((8, 256), 0), iota((8, 256), 1)
    ro = jnp.where(row < 3, 0, 1)
    W["head"][...] = jnp.where(jnp.logical_and(row < 6, ro == lane // 128), t, 0.0).astype(BF)


def prep_all(raw, rawb, W, B, ps):
    prep_bias(rawb, B)
    prep_stem(raw, W, ps)
    prep_plane(raw["outer"], W["outer"], 32, ps)
    prep_corners(raw, W, ps)
    prep_inner(raw["inner"], W["inner"], ps)
    prep_bottom(raw["bottom"], W["bottom"], ps)
    prep_plane(raw["mend"], W["mend"], 64, ps)
    prep_plane(raw["finish"], W["finish"], 32, ps)
    prep_head(raw, W)


MESH = pl.DeviceIdType.MESH


def axis_position():
    return lax.axis_index("sec"), lax.axis_index("gy"), lax.axis_index("gx")


def align(own, left, right, has_left, has_right, cs):
    lane = lax.broadcasted_iota(jnp.int32, (1, 128), 1)

    def shifts(ref, first, ok):
        v = ref[64:80].astype(F32)
        m = jnp.concatenate([jnp.broadcast_to(v[first + i : first + i + 1], (8, 128)) for i in range(8)], axis=0)
        return m if ok is None else jnp.where(ok, m, -1.0)

    pix = [r[0:64].astype(F32) for r in (left, own, right)]
    oy = [shifts(left, 0, has_left), shifts(own, 0, None), shifts(right, 0, has_right)]
    ox = [shifts(left, 8, has_left), shifts(own, 8, None), shifts(right, 8, has_right)]
    rp = [pltpu.roll(p, 16, 1) for p in pix]
    for tile in range(2):
        raw = jnp.where(lane < 16, rp[tile], rp[tile + 1])
        oyt = jnp.where(lane < 16, oy[tile], oy[tile + 1])
        oxt = jnp.where(lane < 16, ox[tile], ox[tile + 1])
        for s in range(5):
            hit = oxt == float(s)
            v = jnp.where(hit, raw, 0.0)
            o = jnp.where(hit, oyt, -1.0)
            cs.vs[s, tile] = v if s == 0 else pltpu.roll(v, s, 1)
            cs.os[s, tile] = o if s == 0 else pltpu.roll(o, s, 1)
    cs.vb[:, :, 0:8] = jnp.zeros((2, 2, 8, 128), F32)
    for tile in range(2):
        total = jnp.zeros((64, 128), F32)
        cover = jnp.zeros((64, 128), F32)
        for t in range(5):
            v = jnp.zeros((64, 128), F32)
            c = jnp.zeros((64, 128), F32)
            for s in range(5):
                vs, os = cs.vs[s, tile], cs.os[s, tile]
                if tile == 1 and s > 0:
                    vs = jnp.where(lane < s, cs.vs[s, 0], vs)
                    os = jnp.where(lane < s, cs.os[s, 0], os)
                hit = os == float(t)
                v = v + jnp.where(hit, vs, 0.0)
                c = c + jnp.where(hit, 1.0, 0.0)
            if t > 0:
                cs.vb[tile, 0, 8:72] = v
                cs.vb[tile, 1, 8:72] = c
                v = cs.vb[tile, 0, 8 - t : 72 - t]
                c = cs.vb[tile, 1, 8 - t : 72 - t]
            total = total + v
            cover = cover + c
        a = (total / jnp.maximum(cover, 1.0)).astype(BF).astype(F32)
        if tile == 0:
            a = jnp.where(jnp.logical_or(lane >= 16, has_left), a, 0.0)
        else:
            a = jnp.where(jnp.logical_or(lane < 16, has_right), a, 0.0)
        a = jnp.concatenate([a, jnp.zeros((64, 128), F32)], axis=0)
        cs.tt[tile * 128 : (tile + 1) * 128] = a.T
    xs = [cs.tt[pl.ds(4 + i, 48, 4), :] for i in range(4)]
    for g in range(8):
        piece = jnp.zeros((48, 128), F32)
        for i in range(4):
            sh = (32 * i - (8 * g - 12)) % 128
            r = xs[i] if sh == 0 else pltpu.roll(xs[i], sh, 1)
            piece = jnp.where(lane // 32 == i, r, piece)
        cs.sbuf[g] = piece.astype(BF)


CS = dict(
    img=((64, 128), BF),
    off=((2, 8), jnp.int32),
    near=((80, 128), BF),
    rb=((2, 80, 128), BF),
    sbuf=((8, 48, 128), BF),
    rx=((NZ, 48, 128), BF),
    vs=((5, 2, 64, 128), F32),
    os=((5, 2, 64, 128), F32),
    vb=((2, 2, 72, 128), F32),
    tt=((256, 128), F32),
)


def gather(img_copy, off_copy, cs, sems, counts, first):
    send1, recv1, send2, send3, recv2 = sems
    sec, gy, gx = axis_position()
    nsec, ngy, ngx = counts
    one = jnp.int32(1)
    has_left, has_right = gx > 0, gx < ngx - 1
    above, below = sec > 0, sec < nsec - 1
    barrier = pltpu.get_barrier_semaphore()

    def greet(*device):
        pl.semaphore_signal(barrier, inc=1, device_id=device, device_id_type=MESH)

    cs.rx[...] = jnp.zeros((NZ, 48, 128), BF)
    cs.rb[...] = jnp.zeros((2, 80, 128), BF)

    @pl.when(has_left)
    def _():
        greet(sec, gy, gx - 1)

    @pl.when(has_right)
    def _():
        greet(sec, gy, gx + 1)

    for k in range(1, 8):
        greet(sec, lax.rem(gy + k, 8), gx)

    @pl.when(below)
    def _():
        greet(sec + 1, 0 * gy, gx)
        greet(sec + 1, 0 * gy + 1, gx)

    @pl.when(above)
    def _():
        greet(sec - 1, 0 * gy + 6, gx)
        greet(sec - 1, 0 * gy + 7, gx)

    to_up = jnp.logical_and(gy < 2, above)
    to_down = jnp.logical_and(gy >= 6, below)
    expect = 7 + jnp.where(has_left, 1, 0) + jnp.where(has_right, 1, 0) + jnp.where(jnp.logical_or(to_up, to_down), 8, 0)

    img_copy.wait()
    off_copy.wait()

    cs.near[0:64] = cs.img[...]
    sh = cs.off[...].astype(F32)
    r16 = iota((16, 8), 0)
    info = jnp.where(r16 < 8, sh[0:1], sh[1:2])
    info = jnp.sum(jnp.where(r16 % 8 == iota((16, 8), 1), info, 0.0), axis=1, keepdims=True)
    cs.near[64:80] = jnp.broadcast_to(info, (16, 128)).astype(BF)

    pl.semaphore_wait(barrier, expect)

    def near_copy(slot, target):
        return pltpu.make_async_remote_copy(
            src_ref=cs.near, dst_ref=cs.rb.at[slot], send_sem=send1.at[slot], recv_sem=recv1.at[slot],
            device_id=(sec, gy, target), device_id_type=MESH,
        )

    @pl.when(has_right)
    def _():
        near_copy(0, gx + 1).start()

    @pl.when(has_left)
    def _():
        near_copy(1, gx - 1).start()

    first()

    @pl.when(has_left)
    def _():
        near_copy(0, gx - 1).wait_recv()

    @pl.when(has_right)
    def _():
        near_copy(1, gx + 1).wait_recv()

    align(cs.near, cs.rb.at[0], cs.rb.at[1], has_left, has_right, cs)

    def far(g, slot, s, sem):
        return pltpu.make_async_remote_copy(
            src_ref=cs.sbuf.at[g], dst_ref=cs.rx.at[slot], send_sem=sem.at[g], recv_sem=recv2.at[slot],
            device_id=(s, g, gx), device_id_type=MESH,
        )

    for k in range(1, 8):
        far(lax.rem(gy + k, 8), gy + 2, sec, send2).start()

    @pl.when(to_up)
    def _():
        for k in range(8):
            far(lax.rem(gy + k, 8), gy + 10, sec - 1, send3).start()

    @pl.when(to_down)
    def _():
        for k in range(8):
            far(lax.rem(gy + k, 8), gy - 6, sec + 1, send3).start()

    cs.rx[gy + 2] = cs.sbuf[gy]

    def finish():
        for k in range(1, 8):
            far(lax.rem(gy + k, 8), 2 + lax.rem(gy + k, 8), sec, send2).wait_recv()

        @pl.when(above)
        def _():
            for slot in (0, 1):
                far(lax.rem(gy + 1, 8), slot, sec - 1, send3).wait_recv()

        @pl.when(below)
        def _():
            for slot in (10, 11):
                far(lax.rem(gy + 1, 8), slot, sec + 1, send3).wait_recv()

    def drain():
        @pl.when(has_right)
        def _():
            near_copy(0, gx + 1).wait_send()

        @pl.when(has_left)
        def _():
            near_copy(1, gx - 1).wait_send()

        for k in range(1, 8):
            far(lax.rem(gy + k, 8), gy + 2, sec, send2).wait_send()

        @pl.when(to_up)
        def _():
            for k in range(8):
                far(lax.rem(gy + k, 8), gy + 10, sec - 1, send3).wait_send()

        @pl.when(to_down)
        def _():
            for k in range(8):
                far(lax.rem(gy + k, 8), gy - 6, sec + 1, send3).wait_send()

    return finish, drain


def fused_call(images, offsets, raw, rawb, counts):
    nin = 2 + len(RAW) + len(RAWB)

    def body(*refs):
        ins, out, rest = refs[:nin], refs[nin], refs[nin + 1 :]

        def take(names):
            nonlocal rest
            head, rest = rest[: len(names)], rest[len(names) :]
            return head

        cs = Refs(CS, take(CS))
        sc = Refs(SCRATCH, take(SCRATCH))
        ps = Refs(PS, take(PS))
        W = dict(zip(WS, take(WS)))
        B = dict(zip(BS, take(BS)))
        R = dict(zip(RAW, take(RAW)))
        RB = dict(zip(RAWB, take(RAWB)))
        load = rest[0]
        sems = rest[1:]
        targets = [cs.img, cs.off] + list(R.values()) + list(RB.values())
        copies = [pltpu.make_async_copy(s, t, load.at[n]) for n, (s, t) in enumerate(zip(ins, targets))]
        for c in copies:
            c.start()

        def first():
            for c in copies[2:]:
                c.wait()
            prep_bias(RB, B)
            prep_stem(R, W, ps)
            prep_plane(R["outer"], W["outer"], 32, ps)

        finish, drain = gather(copies[0], copies[1], cs, sems, counts, first)
        prep_corners(R, W, ps)
        prep_inner(R["inner"], W["inner"], ps)
        prep_bottom(R["bottom"], W["bottom"], ps)
        prep_plane(R["mend"], W["mend"], 64, ps)
        prep_plane(R["finish"], W["finish"], 32, ps)
        prep_head(R, W)
        finish()
        drain()
        compute(axis_position(), counts, cs.rx, W, B, out, sc)

    dma = pltpu.SemaphoreType.DMA
    scratch = list(CS.values()) + list(SCRATCH.values()) + list(PS.values()) + list(WS.values())
    scratch += [(s, F32) for s in BS.values()] + [(s, BF) for s in RAW.values()]
    scratch += [((1, n), F32) for n in RAWB.values()]
    return pl.pallas_call(
        body,
        out_shape=jax.ShapeDtypeStruct((3, 8, 8, 128), F32),
        in_specs=[pl.BlockSpec(memory_space=pl.ANY)] * nin,
        out_specs=pl.BlockSpec(memory_space=pltpu.VMEM),
        scratch_shapes=[pltpu.VMEM(s, t) for s, t in scratch]
        + [dma((nin,)), dma((2,)), dma((2,)), dma((8,)), dma((8,)), dma((12,))],
        compiler_params=pltpu.CompilerParams(
            vmem_limit_bytes=62 * 1024 * 1024, collective_id=0, has_side_effects=True
        ),
    )(images, offsets, *[raw[k] for k in RAW], *[rawb[k] for k in RAWB])


NAMES = (
    "images", "offsets", "stem_kernel", "stem_bias", "outer_kernel", "outer_bias", "pooling_kernel",
    "pooling_bias", "inner_kernel", "inner_bias", "narrowing_kernel", "narrowing_bias", "bottom_kernel",
    "bottom_bias", "lift_kernel", "lift_bias", "mend_kernel", "mend_bias", "expand_kernel", "expand_bias",
    "finish_kernel", "finish_bias", "head_kernel", "head_bias",
)


def solution(mesh):
    counts = (mesh.shape["sec"], mesh.shape["gy"], mesh.shape["gx"])

    def per_device(*args):
        w = dict(zip(NAMES, args))
        raw, rawb = raw_views(w)
        offsets = w["offsets"][0, :, :, 0].T
        logits = fused_call(w["images"].reshape(64, 128), offsets, raw, rawb, counts)
        return jax.nn.sigmoid(logits + w["head_bias"][:, None, None, None])

    in_specs = (P(("sec", "gy"), None, "gx"), P(("sec", "gy"), None, None, "gx")) + (P(),) * 22
    out_specs = P(None, "sec", "gy", "gx")
    return jax.shard_map(per_device, mesh=mesh, in_specs=in_specs, out_specs=out_specs, check_vma=False)
```

```python
import jax
import jax.numpy as jnp
from jax import lax
from jax.experimental import pallas as pl
from jax.experimental.pallas import tpu as pltpu
from jax.sharding import PartitionSpec as P

BF = jnp.bfloat16
F32 = jnp.float32
PITCH = 40
NZ = 12
OUTER_GROUP, INNER_GROUP = 14, 3
R12, R10, R8 = NZ * PITCH, 10 * PITCH, 8 * PITCH
PAD = 16


WN = ("stem", "outer", "pool", "inner", "narrow", "bottom", "lift", "mend", "expand", "finish", "head")
BN = ("stem", "outer", "pool", "inner", "narrow", "bottom", "lift", "mend", "expand", "finish")


def dot(a, b):
    return jnp.dot(a, b, preferred_element_type=F32)


def compute(pos, counts, x4, W, B, out, sc):
    sec, gy, gx = pos
    nsec, ngy, ngx = counts
    lane = lax.broadcasted_iota(jnp.int32, (1, 128), 1)
    rows = lax.broadcasted_iota(jnp.int32, (R12, 1), 0)
    zi = rows // PITCH
    gi = rows - zi * PITCH
    zglob = sec * 8 - 2 + zi
    zok = jnp.logical_and(zglob >= 0, zglob < nsec * 8)
    gg = gx * 32 - 3 + gi

    def gok(shift):
        return jnp.logical_and(gg + shift >= 0, gg + shift < ngx * 32)

    m = jnp.broadcast_to(jnp.where(jnp.logical_and(zok, gok(0)), 1.0, 0.0), (R12, 128))
    sc.mask[0] = jnp.zeros((R12, 128), F32)
    sc.mask[1] = m
    sc.smask[0] = jnp.zeros((R12, 128), BF)
    sc.smask[1] = m.astype(BF)
    right = jnp.where(gok(1), 1.0, 0.0)
    left = jnp.where(gok(-1), 1.0, 0.0)
    zero = jnp.zeros((R12, 1), F32)
    for va in range(2):
        for vb in range(2):
            ra, la = (right, left) if va else (zero, zero)
            rb, lb = (right, left) if vb else (zero, zero)
            e = jnp.where(lane < 32, ra, jnp.where(lane < 64, lb, jnp.where(lane < 96, rb, la)))
            sc.emask[2 * va + vb] = e.astype(BF)

    def rowok(row, total):
        return jnp.where(jnp.logical_and(row >= 0, row < total), 1, 0)

    sc.xf[0:PAD] = jnp.zeros((PAD, 128), F32)
    sc.xf[PAD + R12 :] = jnp.zeros((PAD, 128), F32)
    for z in range(NZ):
        sc.xf[PAD + z * PITCH : PAD + (z + 1) * PITCH] = x4[z, 0:PITCH].astype(F32)
    sc.xin[:, 0:128] = sc.xf[PAD : PAD + R12].astype(BF)
    sc.xin[:, 128:256] = jnp.where(
        lane < 64, sc.xf[PAD + 1 : PAD + 1 + R12], sc.xf[PAD - 1 : PAD - 1 + R12]
    ).astype(BF)

    zero_bf = jnp.zeros((), BF)

    for q in range(15):
        acc = dot(sc.xin[...], W["stem"][q]) + B["stem"][...]
        s = acc.astype(BF)
        va = rowok(gy * 8 + 2 * q - 11, ngy * 8)
        vb = rowok(gy * 8 + 2 * q - 10, ngy * 8)
        sc.se[q] = s[:, 0:128]
        sc.so[q] = s[:, 128:256]
        r = jnp.maximum(s, zero_bf)
        sc.re[q] = r[:, 0:128] * sc.smask[va]
        sc.ro[q] = r[:, 128:256] * sc.smask[vb]
        sc.e[q] = r[:, 256:384] * sc.emask[2 * va + vb]

    def flat(ref, start, count, *rest):
        v = ref[(pl.ds(start, count),) + rest]
        return v.reshape(count * v.shape[1], v.shape[2])

    sc.pf[:, 0:PAD] = jnp.zeros((14, PAD, 128), F32)
    sc.pf[:, PAD + R12 :] = jnp.zeros((14, PAD, 128), F32)

    NP = OUTER_GROUP

    def outer(c, _):
        p = c * NP
        lhs = jnp.concatenate(
            [flat(x, p + h, NP) for h in range(2) for x in (sc.re, sc.ro)] + [flat(sc.e, p, NP), flat(sc.e, p + 1, NP)],
            axis=1,
        )
        acc = dot(lhs, W["outer"][...])
        res = jnp.concatenate([flat(sc.so, p, NP), flat(sc.se, p + 1, NP)], axis=1).astype(F32)
        o = (acc + res + B["outer"][...]).astype(BF)
        for i in range(NP):
            @pl.when(jnp.logical_and(p + i >= 4, p + i < 10))
            def _():
                sc.o[p + i - 4] = o[i * R12 + 80 : i * R12 + 400]
        pooled = (dot(o, W["pool"][...]) + B["pool"][...]).astype(BF).astype(F32)
        for i in range(NP):
            v = rowok(gy * 4 + p + i - 5, ngy * 4)
            sc.pf[p + i, PAD : PAD + R12] = pooled[i * R12 : (i + 1) * R12] * sc.mask[v]
        for i in range(NP):
            q = p + i
            relu = lambda v: jnp.maximum(v, 0.0).astype(BF)
            sc.pa[q, :, 0:128] = relu(sc.pf[q, PAD : PAD + R12])
            ea = jnp.where(lane < 64, sc.pf[q, PAD + 1 : PAD + 1 + R12], sc.pf[q, PAD - 1 : PAD - 1 + R12])
            sc.pa[q, :, 128:256] = relu(ea)
            sc.pb[q, :, 0:128] = relu(sc.pf[q, PAD - 8 : PAD + 8 + R12])
            eb = jnp.where(lane < 64, sc.pf[q, PAD - 7 : PAD + 9 + R12], sc.pf[q, PAD - 9 : PAD + 7 + R12])
            sc.pb[q, :, 128:256] = relu(eb)
        return 0

    lax.fori_loop(0, 14 // NP, outer, 0)

    sc.qf[:, 0:PAD] = jnp.zeros((6, PAD, 128), F32)
    sc.qf[:, PAD + R10 :] = jnp.zeros((6, PAD, 128), F32)

    NK = INNER_GROUP

    def rows4(get, count):
        return [jnp.concatenate([get(2 * k + r) for k in range(count)], axis=0) for r in range(4)]

    def inner(c, _):
        k0 = c * NK
        pieces = []
        for dz in range(3):
            src = (sc.pa, sc.pb, sc.pa)[dz]
            lo = (0, 48, 80)[dz]
            for half in range(2):
                pieces += rows4(
                    lambda t: src[2 * k0 + t, lo : lo + R10, half * 128 : half * 128 + 128], NK
                )
        acc = dot(jnp.concatenate(pieces, axis=1), W["inner"][...].reshape(3072, 256))
        res = jnp.concatenate(
            [
                jnp.concatenate([sc.pf[2 * (k0 + k) + 1 + h, PAD + 40 : PAD + 440] for k in range(NK)], axis=0)
                for h in range(2)
            ],
            axis=1,
        )
        a = (acc + res + B["inner"][...]).astype(BF)
        for k in range(NK):
            sc.i[k0 + k] = a[k * R10 : (k + 1) * R10].astype(F32)[40:360].astype(BF)
        sq = (dot(a, W["narrow"][...]) + B["narrow"][...]).astype(BF).astype(F32)
        for k in range(NK):
            v = rowok(gy * 2 + k0 + k - 2, ngy * 2)
            sc.qf[k0 + k, PAD : PAD + R10] = sq[k * R10 : (k + 1) * R10] * sc.mask[v, 40:440]
        for k in range(NK):
            for d in range(3):
                sc.qa[k0 + k, :, d * 128 : (d + 1) * 128] = jnp.maximum(
                    sc.qf[k0 + k, PAD - 1 + d : PAD - 1 + d + R10], 0.0
                ).astype(BF)
                sc.qb[k0 + k, :, d * 128 : (d + 1) * 128] = jnp.maximum(
                    sc.qf[k0 + k, PAD - 9 + d : PAD + 7 + d + R10], 0.0
                ).astype(BF)
        return 0

    lax.fori_loop(0, 6 // NK, inner, 0)

    sc.lf[:, 0:PAD] = jnp.zeros((8, PAD, 128), F32)
    sc.lf[:, PAD + R8 :] = jnp.zeros((8, PAD, 128), F32)

    pieces = []
    for dz in range(3):
        src = (sc.qa, sc.qb, sc.qa)[dz]
        lo = (0, 48, 80)[dz]
        pieces += rows4(lambda t: src[t, lo : lo + R8, :], 2)
    acc = dot(jnp.concatenate(pieces, axis=1), W["bottom"][...].reshape(4608, 256))
    res = jnp.concatenate(
        [jnp.concatenate([sc.qf[2 * k + 1 + h, PAD + 40 : PAD + 360] for k in range(2)], axis=0) for h in range(2)],
        axis=1,
    )
    a = (acc + res + B["bottom"][...]).astype(BF)
    a = jnp.concatenate([a[k * R8 : (k + 1) * R8, h * 128 : h * 128 + 128] for k in range(2) for h in range(2)], axis=0)
    up = dot(a, W["lift"][...])
    l = (up + flat(sc.i, 1, 4).astype(F32) + B["lift"][...]).astype(BF).astype(F32)
    for t in range(8):
        y, e = t // 2, t % 2
        v = rowok(gy * 4 + t - 2, ngy * 4)
        sc.lf[t, PAD : PAD + R8] = l[y * R8 : (y + 1) * R8, e * 128 : (e + 1) * 128] * sc.mask[v, 80:400]
    for t in range(8):
        sc.pa[t, 0:R8, 0:128] = jnp.maximum(sc.lf[t, PAD : PAD + R8], 0.0).astype(BF)
        ed = jnp.where(lane < 64, sc.lf[t, PAD + 1 : PAD + 1 + R8], sc.lf[t, PAD - 1 : PAD - 1 + R8])
        sc.pa[t, 0:R8, 128:256] = jnp.maximum(ed, 0.0).astype(BF)

    pieces = rows4(lambda t: sc.pa[t, 0:R8, 0:128], 3) + rows4(lambda t: sc.pa[t, 0:R8, 128:256], 3)
    acc = dot(jnp.concatenate(pieces, axis=1), W["mend"][...])
    res = jnp.concatenate(
        [jnp.concatenate([sc.lf[2 * k + 1 + h, PAD : PAD + R8] for k in range(3)], axis=0) for h in range(2)], axis=1
    )
    a = (acc + res + B["mend"][...]).astype(BF)
    a = jnp.concatenate([a[k * R8 : (k + 1) * R8, h * 128 : h * 128 + 128] for k in range(3) for h in range(2)], axis=0)
    up = dot(a, W["expand"][...])
    x = (up + flat(sc.o, 0, 6).astype(F32) + B["expand"][...]).astype(BF).astype(F32)
    for t in range(1, 11):
        j, e = t // 2, t % 2
        v = rowok(gy * 8 + t - 2, ngy * 8)
        xm = x[j * R8 : (j + 1) * R8, e * 128 : (e + 1) * 128] * sc.mask[v, 80:400]
        sc.pf[t, PAD : PAD + R8] = xm
        sc.re[t, 0:R8] = jnp.maximum(xm, 0.0).astype(BF)
    for u in range(5):
        ta, tb = 2 * u + 1, 2 * u + 2
        ua = jnp.where(lane < 64, sc.pf[ta, PAD + 1 : PAD + 1 + R8], sc.pf[ta, PAD - 1 : PAD - 1 + R8])
        ub = jnp.where(lane < 64, sc.pf[tb, PAD + 1 : PAD + 1 + R8], sc.pf[tb, PAD - 1 : PAD - 1 + R8])
        ub = pltpu.roll(ub, 64, 1)
        e = jnp.where(jnp.logical_and(lane >= 32, lane < 96), ub, ua)
        sc.e[u, 0:R8] = jnp.maximum(e, 0.0).astype(BF)

    pieces = rows4(lambda t: sc.re[t + 1, 0:R8], 4) + [flat(sc.e, 0, 4, slice(0, R8)), flat(sc.e, 1, 4, slice(0, R8))]
    acc = dot(jnp.concatenate(pieces, axis=1), W["finish"][...])
    res = jnp.concatenate(
        [jnp.concatenate([sc.pf[2 * k + 2 + h, PAD : PAD + R8] for k in range(4)], axis=0) for h in range(2)], axis=1
    )
    f = (acc + res + B["finish"][...]).astype(BF).astype(F32)
    for h in range(2):
        for u in range(4):
            sc.f[h, u] = f[u * R8 : (u + 1) * R8, h * 128 : (h + 1) * 128]
    for u in range(4):
        for h in range(2):
            for z in range(8):
                fz = sc.f[h, u, z * PITCH + 3 : z * PITCH + 35]
                for j in range(4):
                    sc.g[u % 2, h, pl.ds(z * 128 + j, 32, 4), :] = jnp.where(lane // 32 == j, fz, 0.0)
        gz = jnp.concatenate([sc.g[u % 2, h] for h in range(2)], axis=1).astype(BF)
        lt = lax.dot_general(W["head"][...], gz, (((1,), (1,)), ((), ())), preferred_element_type=F32)
        for z in range(8):
            for ro in range(2):
                for o in range(3):
                    out[o, z, 2 * u + ro : 2 * u + ro + 1, :] = lt[ro * 3 + o : ro * 3 + o + 1, z * 128 : z * 128 + 128]


SCRATCH = dict(
    mask=((2, R12, 128), F32),
    smask=((2, R12, 128), BF),
    emask=((4, R12, 128), BF),
    xf=((R12 + 2 * PAD, 128), F32),
    xin=((R12, 256), BF),
    se=((15, R12, 128), BF),
    so=((15, R12, 128), BF),
    re=((15, R12, 128), BF),
    ro=((15, R12, 128), BF),
    e=((15, R12, 128), BF),
    o=((6, R8, 256), BF),
    pf=((14, R12 + 2 * PAD, 128), F32),
    pa=((14, R12, 256), BF),
    pb=((14, R12 + 16, 256), BF),
    i=((6, R8, 256), BF),
    qf=((6, R10 + 2 * PAD, 128), F32),
    qa=((6, R10, 384), BF),
    qb=((6, R10 + 16, 384), BF),
    lf=((8, R8 + 2 * PAD, 128), F32),
    f=((2, 4, R8, 128), F32),
    g=((2, 2, 1024, 128), F32),
)


class Refs:
    def __init__(self, names, refs):
        for n, r in zip(names, refs):
            setattr(self, n, r)


WS = dict(
    stem=((15, 256, 384), BF),
    outer=((768, 256), BF),
    pool=((256, 128), BF),
    inner=((3, 1024, 256), BF),
    narrow=((256, 128), BF),
    bottom=((3, 1536, 256), BF),
    lift=((128, 256), BF),
    mend=((1024, 256), BF),
    expand=((128, 256), BF),
    finish=((768, 256), BF),
    head=((8, 256), BF),
)
BS = dict(
    stem=(1, 384), outer=(1, 256), pool=(1, 128), inner=(1, 256), narrow=(1, 128), bottom=(1, 256),
    lift=(1, 256), mend=(1, 256), expand=(1, 256), finish=(1, 256),
)
RAW = dict(
    stem=(3, 3, 32), outer=(3, 3, 32, 32), pool=(32, 2, 2, 64), inner=(3, 3, 3, 4096), narrow=(64, 2, 2, 128),
    bottom=(3, 3, 3, 16384), lift=(64, 2, 2, 128), mend=(3, 3, 64, 64), expand=(32, 2, 2, 64),
    finish=(3, 3, 32, 32), head=(3, 32),
)
RAWB = dict(stem=32, outer=32, pool=64, inner=64, narrow=128, bottom=128, lift=64, mend=64, expand=32, finish=32)
LONG = dict(
    stem="stem", outer="outer", pool="pooling", inner="inner", narrow="narrowing", bottom="bottom", lift="lift",
    mend="mend", expand="expand", finish="finish",
)
PS = dict(
    st=((128 * 8, 128), F32),
    sw=((288, 384), F32),
    tb=((27, 128, 128), BF),
)


def raw_views(w):
    def plane(k):
        return k[:, :, 0].transpose(2, 3, 0, 1)

    def inward(k):
        return k[:, :, 0].transpose(1, 2, 3, 0)

    raw = dict(
        stem=w["stem_kernel"][:, 0, 0].transpose(1, 2, 0),
        outer=plane(w["outer_kernel"]), mend=plane(w["mend_kernel"]), finish=plane(w["finish_kernel"]),
        pool=inward(w["pooling_kernel"]), narrow=inward(w["narrowing_kernel"]),
        lift=inward(w["lift_kernel"]), expand=inward(w["expand_kernel"]),
        inner=w["inner_kernel"], bottom=w["bottom_kernel"], head=w["head_kernel"],
    )
    bias = {k: w[LONG[k] + "_bias"].reshape(1, -1) for k in RAWB}
    return raw, bias


def iota(shape, dim):
    return lax.broadcasted_iota(jnp.int32, shape, dim)


def onehot(cond):
    return jnp.where(cond, 1.0, 0.0).astype(BF)


def prep_bias(raw, B):
    for k, n in RAWB.items():
        v = raw[k][...]
        reps = BS[k][1] // n
        B[k][...] = v if reps == 1 else jnp.concatenate([v] * reps, axis=1)


def prep_stem(raw, W, ps):
    k = jnp.concatenate([raw["stem"][dy].astype(F32) for dy in range(3)] + [jnp.zeros((7, 32), F32)], axis=0)
    e = onehot(iota((32, 384), 0) == iota((32, 384), 1) % 32)
    kt = dot(k.astype(BF), e)
    row, lane = iota((32, 384), 0), iota((32, 384), 1)
    a, r, slot = row // 4, row % 4, lane // 32
    i = jnp.where(a < 6, a, a - 8)
    edge = slot >= 8
    ro = jnp.where(edge, jnp.where(jnp.logical_or(slot == 8, slot == 11), 0, 1), slot // 4)
    j = jnp.where(edge, jnp.where(slot % 2 == 0, 4, -1), slot % 4)
    dy, dx = r - ro, i - j + 1
    ok = jnp.logical_and(jnp.logical_and(dy >= 0, dy < 3), jnp.logical_and(dx >= 0, dx < 3))
    idx = jnp.where(ok, 3 * dy + dx, -1)
    base = jnp.zeros((32, 384), F32)
    for d in range(9):
        base = jnp.where(idx == d, kt[d : d + 1], base)
    ps.sw[...] = jnp.zeros((288, 384), F32)
    for a in range(8):
        ps.sw[32 + a * 32 : 36 + a * 32] = base[4 * a : 4 * a + 4]
    for q in range(15):
        W["stem"][q] = ps.sw[32 - 2 * q : 288 - 2 * q].astype(BF)


def prep_plane(k, W, ch, ps):

    flat = jnp.concatenate([k[dy, dx] for dy in range(3) for dx in range(3)], axis=0)
    e = onehot(iota((128, ch), 0) % ch == iota((128, ch), 1))
    t = lax.dot_general(e, flat, (((1,), (1,)), ((), ())), preferred_element_type=F32).astype(BF)
    n = 9 * ch
    er, el = iota((n, 1152), 0), iota((n, 1152), 1)
    spread = onehot(jnp.logical_and(er // ch == el // 128, er % ch == el % ch))
    t = dot(t, spread).astype(BF)
    blocks = [[t[:, (3 * dy + dx) * 128 : (3 * dy + dx + 1) * 128] for dx in range(3)] for dy in range(3)]
    place_plane(blocks, W, ch)


def place_plane(blocks, W, ch, base=None):
    width = 128 // ch
    row, lane = iota((128, 128), 0), iota((128, 128), 1)
    i, j = row // ch, lane // ch
    zero = jnp.zeros((128, 128), F32)
    b32 = [[b.astype(F32) for b in q] for q in blocks]
    diag = []
    for dy in range(3):
        m = zero
        for dx in range(3):
            m = jnp.where(i - j + 1 == dx, b32[dy][dx], m)
        diag.append(m.astype(BF))
    zb = zero.astype(BF)

    def put(at, ro, v):
        if base is None:
            W[at : at + 128, ro * 128 : (ro + 1) * 128] = v
        else:
            W[base, at : at + 128, ro * 128 : (ro + 1) * 128] = v

    for r in range(4):
        for ro in range(2):
            put(r * 128, ro, diag[r - ro] if 0 <= r - ro < 3 else zb)

    def side(dy, dx):
        if not 0 <= dy < 3:
            return zero
        return jnp.where(j == (width - 1 if dx == 2 else 0), b32[dy][dx], 0.0)

    if ch == 32:
        for h in range(2):
            for ro in range(2):
                a, b = 2 * h - ro, 2 * h + 1 - ro
                v = jnp.where(i == 0, side(a, 2), jnp.where(i == 1, side(b, 0), jnp.where(i == 2, side(b, 2), side(a, 0))))
                put(512 + h * 128, ro, v.astype(BF))
    else:
        for r in range(4):
            for ro in range(2):
                v = jnp.where(i == 0, side(r - ro, 2), side(r - ro, 0))
                put(512 + r * 128, ro, v.astype(BF))


def prep_inner(k, W, ps):
    s = onehot(
        jnp.logical_and(iota((128, 256), 0) // 64 == iota((128, 256), 1) // 128,
                        iota((128, 256), 0) % 64 == iota((128, 256), 1) % 64)
    )
    ra, rl = iota((128, 64), 0), iota((128, 64), 1)
    a = onehot((ra % 64) == 2 * (rl % 32) + rl // 32)

    def plane(zy, _):
        dz = zy // 3
        dy = zy - 3 * dz
        for p in range(32):
            ps.st[p * 8 : p * 8 + 3] = k[dz, dy, :, p * 128 : (p + 1) * 128].astype(F32)
        for dx in range(3):
            m = dot(ps.st[pl.ds(dx, 32, 8), :].astype(BF), s)
            m = jnp.concatenate([m[:, 0:128], m[:, 128:256]], axis=0).astype(BF)
            ps.tb[3 * zy + dx] = dot(a, m).astype(BF)
        return 0

    lax.fori_loop(0, 9, plane, 0)
    for dz in range(3):
        blocks = [[ps.tb[9 * dz + 3 * dy + dx] for dx in range(3)] for dy in range(3)]
        place_plane(blocks, W, 64, base=dz)


def prep_bottom(k, W, ps):
    zb = jnp.zeros((384, 128), BF)
    for dz in range(3):
        W[dz, 0:384, 128:256] = zb
        W[dz, 1152:1536, 0:128] = zb

    def plane(zy, _):
        dz = zy // 3
        dy = zy - 3 * dz
        for c in range(128):
            ps.st[c * 8 : c * 8 + 3] = k[dz, dy, :, c * 128 : (c + 1) * 128].astype(F32)
        for dx in range(3):
            m = ps.st[pl.ds(dx, 128, 8), :].astype(BF)
            W[dz, pl.ds(pl.multiple_of(dy * 384 + dx * 128, 128), 128), 0:128] = m
            W[dz, pl.ds(pl.multiple_of(dy * 384 + 384 + dx * 128, 128), 128), 128:256] = m
        return 0

    lax.fori_loop(0, 9, plane, 0)


def corners(k, ch, ps):
    n = k.shape[3]
    for c in range(ch):
        for p in range(2):
            v = k[c, p].astype(F32)
            ps.st[(2 * c + p) * 8 : (2 * c + p) * 8 + 2, 0:n] = v
    return [[ps.st[pl.ds(8 * p + q, ch, 16), :] for q in range(2)] for p in range(2)]


def prep_corners(raw, W, ps):
    lane = iota((32, 128), 1)
    for name in ("pool", "expand"):
        x = corners(raw[name], 32, ps)
        rows = []
        for p in range(2):
            for i in range(4):
                v = jnp.where(lane < 64, x[p][i % 2], 0.0)
                rows.append(v if i < 2 else pltpu.roll(v, 64, 1))
        z = jnp.concatenate(rows, axis=0)
        if name == "pool":
            W["pool"][...] = z.astype(BF)
        else:
            W["expand"][...] = jnp.concatenate([z[0:128].T, z[128:256].T], axis=1).astype(BF)
    x = corners(raw["narrow"], 64, ps)
    W["narrow"][...] = jnp.concatenate([x[p][q] for p in range(2) for q in range(2)], axis=0).astype(BF)
    x = corners(raw["lift"], 64, ps)
    z = [jnp.concatenate([x[p][0], x[p][1]], axis=0) for p in range(2)]
    W["lift"][...] = jnp.concatenate([z[0].T, z[1].T], axis=1).astype(BF)


def prep_head(raw, W):
    h = raw["head"][...].astype(F32)
    h = jnp.concatenate([h, h, jnp.zeros((2, 32), F32)], axis=0).astype(BF)
    e = onehot(iota((32, 256), 0) == iota((32, 256), 1) % 32)
    t = dot(h, e)
    row, lane = iota((8, 256), 0), iota((8, 256), 1)
    ro = jnp.where(row < 3, 0, 1)
    W["head"][...] = jnp.where(jnp.logical_and(row < 6, ro == lane // 128), t, 0.0).astype(BF)


def prep_all(raw, rawb, W, B, ps):
    prep_bias(rawb, B)
    prep_stem(raw, W, ps)
    prep_plane(raw["outer"], W["outer"], 32, ps)
    prep_corners(raw, W, ps)
    prep_inner(raw["inner"], W["inner"], ps)
    prep_bottom(raw["bottom"], W["bottom"], ps)
    prep_plane(raw["mend"], W["mend"], 64, ps)
    prep_plane(raw["finish"], W["finish"], 32, ps)
    prep_head(raw, W)


MESH = pl.DeviceIdType.MESH


def axis_position():
    return lax.axis_index("sec"), lax.axis_index("gy"), lax.axis_index("gx")


def align(own, left, right, has_left, has_right, cs):
    lane = lax.broadcasted_iota(jnp.int32, (1, 128), 1)

    def shifts(ref, first, ok):
        v = ref[64:80].astype(F32)
        m = jnp.concatenate([jnp.broadcast_to(v[first + i : first + i + 1], (8, 128)) for i in range(8)], axis=0)
        return m if ok is None else jnp.where(ok, m, -1.0)

    pix = [r[0:64].astype(F32) for r in (left, own, right)]
    oy = [shifts(left, 0, has_left), shifts(own, 0, None), shifts(right, 0, has_right)]
    ox = [shifts(left, 8, has_left), shifts(own, 8, None), shifts(right, 8, has_right)]
    rp = [pltpu.roll(p, 16, 1) for p in pix]
    for tile in range(2):
        raw = jnp.where(lane < 16, rp[tile], rp[tile + 1])
        oyt = jnp.where(lane < 16, oy[tile], oy[tile + 1])
        oxt = jnp.where(lane < 16, ox[tile], ox[tile + 1])
        for s in range(5):
            hit = oxt == float(s)
            v = jnp.where(hit, raw, 0.0)
            o = jnp.where(hit, oyt, -1.0)
            cs.vs[s, tile] = v if s == 0 else pltpu.roll(v, s, 1)
            cs.os[s, tile] = o if s == 0 else pltpu.roll(o, s, 1)
    cs.vb[:, :, 0:8] = jnp.zeros((2, 2, 8, 128), F32)
    for tile in range(2):
        total = jnp.zeros((64, 128), F32)
        cover = jnp.zeros((64, 128), F32)
        for t in range(5):
            v = jnp.zeros((64, 128), F32)
            c = jnp.zeros((64, 128), F32)
            for s in range(5):
                vs, os = cs.vs[s, tile], cs.os[s, tile]
                if tile == 1 and s > 0:
                    vs = jnp.where(lane < s, cs.vs[s, 0], vs)
                    os = jnp.where(lane < s, cs.os[s, 0], os)
                hit = os == float(t)
                v = v + jnp.where(hit, vs, 0.0)
                c = c + jnp.where(hit, 1.0, 0.0)
            if t > 0:
                cs.vb[tile, 0, 8:72] = v
                cs.vb[tile, 1, 8:72] = c
                v = cs.vb[tile, 0, 8 - t : 72 - t]
                c = cs.vb[tile, 1, 8 - t : 72 - t]
            total = total + v
            cover = cover + c
        a = (total / jnp.maximum(cover, 1.0)).astype(BF).astype(F32)
        if tile == 0:
            a = jnp.where(jnp.logical_or(lane >= 16, has_left), a, 0.0)
        else:
            a = jnp.where(jnp.logical_or(lane < 16, has_right), a, 0.0)
        a = jnp.concatenate([a, jnp.zeros((64, 128), F32)], axis=0)
        cs.tt[tile * 128 : (tile + 1) * 128] = a.T
    xs = [cs.tt[pl.ds(4 + i, 48, 4), :] for i in range(4)]
    for g in range(8):
        piece = jnp.zeros((48, 128), F32)
        for i in range(4):
            sh = (32 * i - (8 * g - 12)) % 128
            r = xs[i] if sh == 0 else pltpu.roll(xs[i], sh, 1)
            piece = jnp.where(lane // 32 == i, r, piece)
        cs.sbuf[g] = piece.astype(BF)


CS = dict(
    img=((64, 128), BF),
    off=((2, 8), jnp.int32),
    near=((80, 128), BF),
    rb=((2, 80, 128), BF),
    sbuf=((8, 48, 128), BF),
    rx=((NZ, 48, 128), BF),
    vs=((5, 2, 64, 128), F32),
    os=((5, 2, 64, 128), F32),
    vb=((2, 2, 72, 128), F32),
    tt=((256, 128), F32),
)


def gather(img_copy, off_copy, cs, sems, counts, first):
    send1, recv1, send2, send3, recv2 = sems
    sec, gy, gx = axis_position()
    nsec, ngy, ngx = counts
    one = jnp.int32(1)
    has_left, has_right = gx > 0, gx < ngx - 1
    above, below = sec > 0, sec < nsec - 1
    barrier = pltpu.get_barrier_semaphore()

    def greet(*device):
        pl.semaphore_signal(barrier, inc=1, device_id=device, device_id_type=MESH)

    cs.rx[...] = jnp.zeros((NZ, 48, 128), BF)
    cs.rb[...] = jnp.zeros((2, 80, 128), BF)

    @pl.when(has_left)
    def _():
        greet(sec, gy, gx - 1)

    @pl.when(has_right)
    def _():
        greet(sec, gy, gx + 1)

    for k in range(1, 8):
        greet(sec, lax.rem(gy + k, 8), gx)

    @pl.when(below)
    def _():
        greet(sec + 1, 0 * gy, gx)
        greet(sec + 1, 0 * gy + 1, gx)

    @pl.when(above)
    def _():
        greet(sec - 1, 0 * gy + 6, gx)
        greet(sec - 1, 0 * gy + 7, gx)

    to_up = jnp.logical_and(gy < 2, above)
    to_down = jnp.logical_and(gy >= 6, below)
    expect = 7 + jnp.where(has_left, 1, 0) + jnp.where(has_right, 1, 0) + jnp.where(jnp.logical_or(to_up, to_down), 8, 0)

    img_copy.wait()
    off_copy.wait()

    cs.near[0:64] = cs.img[...]
    sh = cs.off[...].astype(F32)
    r16 = iota((16, 8), 0)
    info = jnp.where(r16 < 8, sh[0:1], sh[1:2])
    info = jnp.sum(jnp.where(r16 % 8 == iota((16, 8), 1), info, 0.0), axis=1, keepdims=True)
    cs.near[64:80] = jnp.broadcast_to(info, (16, 128)).astype(BF)

    pl.semaphore_wait(barrier, expect)

    def near_copy(slot, target):
        return pltpu.make_async_remote_copy(
            src_ref=cs.near, dst_ref=cs.rb.at[slot], send_sem=send1.at[slot], recv_sem=recv1.at[slot],
            device_id=(sec, gy, target), device_id_type=MESH,
        )

    @pl.when(has_right)
    def _():
        near_copy(0, gx + 1).start()

    @pl.when(has_left)
    def _():
        near_copy(1, gx - 1).start()

    first()

    @pl.when(has_left)
    def _():
        near_copy(0, gx - 1).wait_recv()

    @pl.when(has_right)
    def _():
        near_copy(1, gx + 1).wait_recv()

    align(cs.near, cs.rb.at[0], cs.rb.at[1], has_left, has_right, cs)

    def far(g, slot, s, sem):
        return pltpu.make_async_remote_copy(
            src_ref=cs.sbuf.at[g], dst_ref=cs.rx.at[slot], send_sem=sem.at[g], recv_sem=recv2.at[slot],
            device_id=(s, g, gx), device_id_type=MESH,
        )

    for k in range(1, 8):
        far(lax.rem(gy + k, 8), gy + 2, sec, send2).start()

    @pl.when(to_up)
    def _():
        for k in range(8):
            far(lax.rem(gy + k, 8), gy + 10, sec - 1, send3).start()

    @pl.when(to_down)
    def _():
        for k in range(8):
            far(lax.rem(gy + k, 8), gy - 6, sec + 1, send3).start()

    cs.rx[gy + 2] = cs.sbuf[gy]

    def finish():
        for k in range(1, 8):
            far(lax.rem(gy + k, 8), 2 + lax.rem(gy + k, 8), sec, send2).wait_recv()

        @pl.when(above)
        def _():
            for slot in (0, 1):
                far(lax.rem(gy + 1, 8), slot, sec - 1, send3).wait_recv()

        @pl.when(below)
        def _():
            for slot in (10, 11):
                far(lax.rem(gy + 1, 8), slot, sec + 1, send3).wait_recv()

    def drain():
        @pl.when(has_right)
        def _():
            near_copy(0, gx + 1).wait_send()

        @pl.when(has_left)
        def _():
            near_copy(1, gx - 1).wait_send()

        for k in range(1, 8):
            far(lax.rem(gy + k, 8), gy + 2, sec, send2).wait_send()

        @pl.when(to_up)
        def _():
            for k in range(8):
                far(lax.rem(gy + k, 8), gy + 10, sec - 1, send3).wait_send()

        @pl.when(to_down)
        def _():
            for k in range(8):
                far(lax.rem(gy + k, 8), gy - 6, sec + 1, send3).wait_send()

    return finish, drain


def fused_call(images, offsets, raw, rawb, counts):
    nin = 2 + len(RAW) + len(RAWB)

    def body(*refs):
        ins, out, rest = refs[:nin], refs[nin], refs[nin + 1 :]

        def take(names):
            nonlocal rest
            head, rest = rest[: len(names)], rest[len(names) :]
            return head

        cs = Refs(CS, take(CS))
        sc = Refs(SCRATCH, take(SCRATCH))
        ps = Refs(PS, take(PS))
        W = dict(zip(WS, take(WS)))
        B = dict(zip(BS, take(BS)))
        R = dict(zip(RAW, take(RAW)))
        RB = dict(zip(RAWB, take(RAWB)))
        load = rest[0]
        sems = rest[1:]
        targets = [cs.img, cs.off] + list(R.values()) + list(RB.values())
        copies = [pltpu.make_async_copy(s, t, load.at[n]) for n, (s, t) in enumerate(zip(ins, targets))]
        for c in copies:
            c.start()

        def first():
            for c in copies[2:]:
                c.wait()
            prep_bias(RB, B)
            prep_stem(R, W, ps)
            prep_plane(R["outer"], W["outer"], 32, ps)

        finish, drain = gather(copies[0], copies[1], cs, sems, counts, first)
        prep_corners(R, W, ps)
        prep_inner(R["inner"], W["inner"], ps)
        prep_bottom(R["bottom"], W["bottom"], ps)
        prep_plane(R["mend"], W["mend"], 64, ps)
        prep_plane(R["finish"], W["finish"], 32, ps)
        prep_head(R, W)
        finish()
        drain()
        compute(axis_position(), counts, cs.rx, W, B, out, sc)

    dma = pltpu.SemaphoreType.DMA
    scratch = list(CS.values()) + list(SCRATCH.values()) + list(PS.values()) + list(WS.values())
    scratch += [(s, F32) for s in BS.values()] + [(s, BF) for s in RAW.values()]
    scratch += [((1, n), F32) for n in RAWB.values()]
    return pl.pallas_call(
        body,
        out_shape=jax.ShapeDtypeStruct((3, 8, 8, 128), F32),
        in_specs=[pl.BlockSpec(memory_space=pl.ANY)] * nin,
        out_specs=pl.BlockSpec(memory_space=pltpu.VMEM),
        scratch_shapes=[pltpu.VMEM(s, t) for s, t in scratch]
        + [dma((nin,)), dma((2,)), dma((2,)), dma((8,)), dma((8,)), dma((12,))],
        compiler_params=pltpu.CompilerParams(
            vmem_limit_bytes=62 * 1024 * 1024, collective_id=0, has_side_effects=True
        ),
    )(images, offsets, *[raw[k] for k in RAW], *[rawb[k] for k in RAWB])


NAMES = (
    "images", "offsets", "stem_kernel", "stem_bias", "outer_kernel", "outer_bias", "pooling_kernel",
    "pooling_bias", "inner_kernel", "inner_bias", "narrowing_kernel", "narrowing_bias", "bottom_kernel",
    "bottom_bias", "lift_kernel", "lift_bias", "mend_kernel", "mend_bias", "expand_kernel", "expand_bias",
    "finish_kernel", "finish_bias", "head_kernel", "head_bias",
)


def solution(mesh):
    counts = (mesh.shape["sec"], mesh.shape["gy"], mesh.shape["gx"])

    def per_device(*args):
        w = dict(zip(NAMES, args))
        raw, rawb = raw_views(w)
        offsets = w["offsets"][0, :, :, 0].T
        logits = fused_call(w["images"].reshape(64, 128), offsets, raw, rawb, counts)
        return jax.nn.sigmoid(logits + w["head_bias"][:, None, None, None])

    in_specs = (P(("sec", "gy"), None, "gx"), P(("sec", "gy"), None, None, "gx")) + (P(),) * 22
    out_specs = P(None, "sec", "gy", "gx")
    return jax.shard_map(per_device, mesh=mesh, in_specs=in_specs, out_specs=out_specs, check_vma=False)
```

```python
import jax
import jax.numpy as jnp
from jax import lax
from jax.experimental import pallas as pl
from jax.experimental.pallas import tpu as pltpu
from jax.sharding import PartitionSpec as P

BF = jnp.bfloat16
F32 = jnp.float32
PITCH = 40
NZ = 12
OUTER_GROUP, INNER_GROUP = 14, 3
R12, R10, R8 = NZ * PITCH, 10 * PITCH, 8 * PITCH
PAD = 16


WN = ("stem", "outer", "pool", "inner", "narrow", "bottom", "lift", "mend", "expand", "finish", "head")
BN = ("stem", "outer", "pool", "inner", "narrow", "bottom", "lift", "mend", "expand", "finish")


def dot(a, b):
    return jnp.dot(a, b, preferred_element_type=F32)


def compute(pos, counts, x4, W, B, out, sc):
    sec, gy, gx = pos
    nsec, ngy, ngx = counts
    lane = lax.broadcasted_iota(jnp.int32, (1, 128), 1)
    rows = lax.broadcasted_iota(jnp.int32, (R12, 1), 0)
    zi = rows // PITCH
    gi = rows - zi * PITCH
    zglob = sec * 8 - 2 + zi
    zok = jnp.logical_and(zglob >= 0, zglob < nsec * 8)
    gg = gx * 32 - 3 + gi

    def gok(shift):
        return jnp.logical_and(gg + shift >= 0, gg + shift < ngx * 32)

    m = jnp.broadcast_to(jnp.where(jnp.logical_and(zok, gok(0)), 1.0, 0.0), (R12, 128))
    sc.mask[0] = jnp.zeros((R12, 128), F32)
    sc.mask[1] = m
    sc.smask[0] = jnp.zeros((R12, 128), BF)
    sc.smask[1] = m.astype(BF)
    right = jnp.where(gok(1), 1.0, 0.0)
    left = jnp.where(gok(-1), 1.0, 0.0)
    zero = jnp.zeros((R12, 1), F32)
    for va in range(2):
        for vb in range(2):
            ra, la = (right, left) if va else (zero, zero)
            rb, lb = (right, left) if vb else (zero, zero)
            e = jnp.where(lane < 32, ra, jnp.where(lane < 64, lb, jnp.where(lane < 96, rb, la)))
            sc.emask[2 * va + vb] = e.astype(BF)

    def rowok(row, total):
        return jnp.where(jnp.logical_and(row >= 0, row < total), 1, 0)

    sc.xf[0:PAD] = jnp.zeros((PAD, 128), F32)
    sc.xf[PAD + R12 :] = jnp.zeros((PAD, 128), F32)
    for z in range(NZ):
        sc.xf[PAD + z * PITCH : PAD + (z + 1) * PITCH] = x4[z, 0:PITCH].astype(F32)
    sc.xin[:, 0:128] = sc.xf[PAD : PAD + R12].astype(BF)
    sc.xin[:, 128:256] = jnp.where(
        lane < 64, sc.xf[PAD + 1 : PAD + 1 + R12], sc.xf[PAD - 1 : PAD - 1 + R12]
    ).astype(BF)

    zero_bf = jnp.zeros((), BF)

    for q in range(15):
        acc = dot(sc.xin[...], W["stem"][q]) + B["stem"][...]
        s = acc.astype(BF)
        va = rowok(gy * 8 + 2 * q - 11, ngy * 8)
        vb = rowok(gy * 8 + 2 * q - 10, ngy * 8)
        sc.se[q] = s[:, 0:128]
        sc.so[q] = s[:, 128:256]
        r = jnp.maximum(s, zero_bf)
        sc.re[q] = r[:, 0:128] * sc.smask[va]
        sc.ro[q] = r[:, 128:256] * sc.smask[vb]
        sc.e[q] = r[:, 256:384] * sc.emask[2 * va + vb]

    def flat(ref, start, count, *rest):
        v = ref[(pl.ds(start, count),) + rest]
        return v.reshape(count * v.shape[1], v.shape[2])

    sc.pf[:, 0:PAD] = jnp.zeros((14, PAD, 128), F32)
    sc.pf[:, PAD + R12 :] = jnp.zeros((14, PAD, 128), F32)

    NP = OUTER_GROUP

    def outer(c, _):
        p = c * NP
        lhs = jnp.concatenate(
            [flat(x, p + h, NP) for h in range(2) for x in (sc.re, sc.ro)] + [flat(sc.e, p, NP), flat(sc.e, p + 1, NP)],
            axis=1,
        )
        acc = dot(lhs, W["outer"][...])
        res = jnp.concatenate([flat(sc.so, p, NP), flat(sc.se, p + 1, NP)], axis=1).astype(F32)
        o = (acc + res + B["outer"][...]).astype(BF)
        for i in range(NP):
            @pl.when(jnp.logical_and(p + i >= 4, p + i < 10))
            def _():
                sc.o[p + i - 4] = o[i * R12 + 80 : i * R12 + 400]
        pooled = (dot(o, W["pool"][...]) + B["pool"][...]).astype(BF).astype(F32)
        for i in range(NP):
            v = rowok(gy * 4 + p + i - 5, ngy * 4)
            sc.pf[p + i, PAD : PAD + R12] = pooled[i * R12 : (i + 1) * R12] * sc.mask[v]
        for i in range(NP):
            q = p + i
            relu = lambda v: jnp.maximum(v, 0.0).astype(BF)
            sc.pa[q, :, 0:128] = relu(sc.pf[q, PAD : PAD + R12])
            ea = jnp.where(lane < 64, sc.pf[q, PAD + 1 : PAD + 1 + R12], sc.pf[q, PAD - 1 : PAD - 1 + R12])
            sc.pa[q, :, 128:256] = relu(ea)
            sc.pb[q, :, 0:128] = relu(sc.pf[q, PAD - 8 : PAD + 8 + R12])
            eb = jnp.where(lane < 64, sc.pf[q, PAD - 7 : PAD + 9 + R12], sc.pf[q, PAD - 9 : PAD + 7 + R12])
            sc.pb[q, :, 128:256] = relu(eb)
        return 0

    lax.fori_loop(0, 14 // NP, outer, 0)

    sc.qf[:, 0:PAD] = jnp.zeros((6, PAD, 128), F32)
    sc.qf[:, PAD + R10 :] = jnp.zeros((6, PAD, 128), F32)

    NK = INNER_GROUP

    def rows4(get, count):
        return [jnp.concatenate([get(2 * k + r) for k in range(count)], axis=0) for r in range(4)]

    def inner(c, _):
        k0 = c * NK
        pieces = []
        for dz in range(3):
            src = (sc.pa, sc.pb, sc.pa)[dz]
            lo = (0, 48, 80)[dz]
            for half in range(2):
                pieces += rows4(
                    lambda t: src[2 * k0 + t, lo : lo + R10, half * 128 : half * 128 + 128], NK
                )
        acc = dot(jnp.concatenate(pieces, axis=1), W["inner"][...].reshape(3072, 256))
        res = jnp.concatenate(
            [
                jnp.concatenate([sc.pf[2 * (k0 + k) + 1 + h, PAD + 40 : PAD + 440] for k in range(NK)], axis=0)
                for h in range(2)
            ],
            axis=1,
        )
        a = (acc + res + B["inner"][...]).astype(BF)
        for k in range(NK):
            sc.i[k0 + k] = a[k * R10 : (k + 1) * R10].astype(F32)[40:360].astype(BF)
        sq = (dot(a, W["narrow"][...]) + B["narrow"][...]).astype(BF).astype(F32)
        for k in range(NK):
            v = rowok(gy * 2 + k0 + k - 2, ngy * 2)
            sc.qf[k0 + k, PAD : PAD + R10] = sq[k * R10 : (k + 1) * R10] * sc.mask[v, 40:440]
        for k in range(NK):
            for d in range(3):
                sc.qa[k0 + k, :, d * 128 : (d + 1) * 128] = jnp.maximum(
                    sc.qf[k0 + k, PAD - 1 + d : PAD - 1 + d + R10], 0.0
                ).astype(BF)
                sc.qb[k0 + k, :, d * 128 : (d + 1) * 128] = jnp.maximum(
                    sc.qf[k0 + k, PAD - 9 + d : PAD + 7 + d + R10], 0.0
                ).astype(BF)
        return 0

    lax.fori_loop(0, 6 // NK, inner, 0)

    sc.lf[:, 0:PAD] = jnp.zeros((8, PAD, 128), F32)
    sc.lf[:, PAD + R8 :] = jnp.zeros((8, PAD, 128), F32)

    pieces = []
    for dz in range(3):
        src = (sc.qa, sc.qb, sc.qa)[dz]
        lo = (0, 48, 80)[dz]
        pieces += rows4(lambda t: src[t, lo : lo + R8, :], 2)
    acc = dot(jnp.concatenate(pieces, axis=1), W["bottom"][...].reshape(4608, 256))
    res = jnp.concatenate(
        [jnp.concatenate([sc.qf[2 * k + 1 + h, PAD + 40 : PAD + 360] for k in range(2)], axis=0) for h in range(2)],
        axis=1,
    )
    a = (acc + res + B["bottom"][...]).astype(BF)
    a = jnp.concatenate([a[k * R8 : (k + 1) * R8, h * 128 : h * 128 + 128] for k in range(2) for h in range(2)], axis=0)
    up = dot(a, W["lift"][...])
    l = (up + flat(sc.i, 1, 4).astype(F32) + B["lift"][...]).astype(BF).astype(F32)
    for t in range(8):
        y, e = t // 2, t % 2
        v = rowok(gy * 4 + t - 2, ngy * 4)
        sc.lf[t, PAD : PAD + R8] = l[y * R8 : (y + 1) * R8, e * 128 : (e + 1) * 128] * sc.mask[v, 80:400]
    for t in range(8):
        sc.pa[t, 0:R8, 0:128] = jnp.maximum(sc.lf[t, PAD : PAD + R8], 0.0).astype(BF)
        ed = jnp.where(lane < 64, sc.lf[t, PAD + 1 : PAD + 1 + R8], sc.lf[t, PAD - 1 : PAD - 1 + R8])
        sc.pa[t, 0:R8, 128:256] = jnp.maximum(ed, 0.0).astype(BF)

    pieces = rows4(lambda t: sc.pa[t, 0:R8, 0:128], 3) + rows4(lambda t: sc.pa[t, 0:R8, 128:256], 3)
    acc = dot(jnp.concatenate(pieces, axis=1), W["mend"][...])
    res = jnp.concatenate(
        [jnp.concatenate([sc.lf[2 * k + 1 + h, PAD : PAD + R8] for k in range(3)], axis=0) for h in range(2)], axis=1
    )
    a = (acc + res + B["mend"][...]).astype(BF)
    a = jnp.concatenate([a[k * R8 : (k + 1) * R8, h * 128 : h * 128 + 128] for k in range(3) for h in range(2)], axis=0)
    up = dot(a, W["expand"][...])
    x = (up + flat(sc.o, 0, 6).astype(F32) + B["expand"][...]).astype(BF).astype(F32)
    for t in range(1, 11):
        j, e = t // 2, t % 2
        v = rowok(gy * 8 + t - 2, ngy * 8)
        xm = x[j * R8 : (j + 1) * R8, e * 128 : (e + 1) * 128] * sc.mask[v, 80:400]
        sc.pf[t, PAD : PAD + R8] = xm
        sc.re[t, 0:R8] = jnp.maximum(xm, 0.0).astype(BF)
    for u in range(5):
        ta, tb = 2 * u + 1, 2 * u + 2
        ua = jnp.where(lane < 64, sc.pf[ta, PAD + 1 : PAD + 1 + R8], sc.pf[ta, PAD - 1 : PAD - 1 + R8])
        ub = jnp.where(lane < 64, sc.pf[tb, PAD + 1 : PAD + 1 + R8], sc.pf[tb, PAD - 1 : PAD - 1 + R8])
        ub = pltpu.roll(ub, 64, 1)
        e = jnp.where(jnp.logical_and(lane >= 32, lane < 96), ub, ua)
        sc.e[u, 0:R8] = jnp.maximum(e, 0.0).astype(BF)

    pieces = rows4(lambda t: sc.re[t + 1, 0:R8], 4) + [flat(sc.e, 0, 4, slice(0, R8)), flat(sc.e, 1, 4, slice(0, R8))]
    acc = dot(jnp.concatenate(pieces, axis=1), W["finish"][...])
    res = jnp.concatenate(
        [jnp.concatenate([sc.pf[2 * k + 2 + h, PAD : PAD + R8] for k in range(4)], axis=0) for h in range(2)], axis=1
    )
    f = (acc + res + B["finish"][...]).astype(BF).astype(F32)
    for h in range(2):
        for u in range(4):
            sc.f[h, u] = f[u * R8 : (u + 1) * R8, h * 128 : (h + 1) * 128]
    for u in range(4):
        for h in range(2):
            for z in range(8):
                fz = sc.f[h, u, z * PITCH + 3 : z * PITCH + 35]
                for j in range(4):
                    sc.g[u % 2, h, pl.ds(z * 128 + j, 32, 4), :] = jnp.where(lane // 32 == j, fz, 0.0)
        gz = jnp.concatenate([sc.g[u % 2, h] for h in range(2)], axis=1).astype(BF)
        lt = lax.dot_general(W["head"][...], gz, (((1,), (1,)), ((), ())), preferred_element_type=F32)
        for z in range(8):
            for ro in range(2):
                for o in range(3):
                    out[o, z, 2 * u + ro : 2 * u + ro + 1, :] = lt[ro * 3 + o : ro * 3 + o + 1, z * 128 : z * 128 + 128]


SCRATCH = dict(
    mask=((2, R12, 128), F32),
    smask=((2, R12, 128), BF),
    emask=((4, R12, 128), BF),
    xf=((R12 + 2 * PAD, 128), F32),
    xin=((R12, 256), BF),
    se=((15, R12, 128), BF),
    so=((15, R12, 128), BF),
    re=((15, R12, 128), BF),
    ro=((15, R12, 128), BF),
    e=((15, R12, 128), BF),
    o=((6, R8, 256), BF),
    pf=((14, R12 + 2 * PAD, 128), F32),
    pa=((14, R12, 256), BF),
    pb=((14, R12 + 16, 256), BF),
    i=((6, R8, 256), BF),
    qf=((6, R10 + 2 * PAD, 128), F32),
    qa=((6, R10, 384), BF),
    qb=((6, R10 + 16, 384), BF),
    lf=((8, R8 + 2 * PAD, 128), F32),
    f=((2, 4, R8, 128), F32),
    g=((2, 2, 1024, 128), F32),
)


class Refs:
    def __init__(self, names, refs):
        for n, r in zip(names, refs):
            setattr(self, n, r)


WS = dict(
    stem=((15, 256, 384), BF),
    outer=((768, 256), BF),
    pool=((256, 128), BF),
    inner=((3, 1024, 256), BF),
    narrow=((256, 128), BF),
    bottom=((3, 1536, 256), BF),
    lift=((128, 256), BF),
    mend=((1024, 256), BF),
    expand=((128, 256), BF),
    finish=((768, 256), BF),
    head=((8, 256), BF),
)
BS = dict(
    stem=(1, 384), outer=(1, 256), pool=(1, 128), inner=(1, 256), narrow=(1, 128), bottom=(1, 256),
    lift=(1, 256), mend=(1, 256), expand=(1, 256), finish=(1, 256),
)
RAW = dict(
    stem=(3, 3, 32), outer=(3, 3, 32, 32), pool=(32, 2, 2, 64), inner=(3, 3, 3, 4096), narrow=(64, 2, 2, 128),
    bottom=(3, 3, 3, 16384), lift=(64, 2, 2, 128), mend=(3, 3, 64, 64), expand=(32, 2, 2, 64),
    finish=(3, 3, 32, 32), head=(3, 32),
)
RAWB = dict(stem=32, outer=32, pool=64, inner=64, narrow=128, bottom=128, lift=64, mend=64, expand=32, finish=32)
LONG = dict(
    stem="stem", outer="outer", pool="pooling", inner="inner", narrow="narrowing", bottom="bottom", lift="lift",
    mend="mend", expand="expand", finish="finish",
)
PS = dict(
    st=((128 * 8, 128), F32),
    sw=((288, 384), F32),
    ma=((864, 128), BF),
    mb=((864, 256), BF),
)


def raw_views(w):
    def plane(k):
        return k[:, :, 0].transpose(2, 3, 0, 1)

    def inward(k):
        return k[:, :, 0].transpose(1, 2, 3, 0)

    raw = dict(
        stem=w["stem_kernel"][:, 0, 0].transpose(1, 2, 0),
        outer=plane(w["outer_kernel"]), mend=plane(w["mend_kernel"]), finish=plane(w["finish_kernel"]),
        pool=inward(w["pooling_kernel"]), narrow=inward(w["narrowing_kernel"]),
        lift=inward(w["lift_kernel"]), expand=inward(w["expand_kernel"]),
        inner=w["inner_kernel"], bottom=w["bottom_kernel"], head=w["head_kernel"],
    )
    bias = {k: w[LONG[k] + "_bias"].reshape(1, -1) for k in RAWB}
    return raw, bias


def iota(shape, dim):
    return lax.broadcasted_iota(jnp.int32, shape, dim)


def onehot(cond):
    return jnp.where(cond, 1.0, 0.0).astype(BF)


def prep_bias(raw, B):
    for k, n in RAWB.items():
        v = raw[k][...]
        reps = BS[k][1] // n
        B[k][...] = v if reps == 1 else jnp.concatenate([v] * reps, axis=1)


def prep_stem(raw, W, ps):
    k = jnp.concatenate([raw["stem"][dy].astype(F32) for dy in range(3)] + [jnp.zeros((7, 32), F32)], axis=0)
    e = onehot(iota((32, 384), 0) == iota((32, 384), 1) % 32)
    kt = dot(k.astype(BF), e)
    row, lane = iota((32, 384), 0), iota((32, 384), 1)
    a, r, slot = row // 4, row % 4, lane // 32
    i = jnp.where(a < 6, a, a - 8)
    edge = slot >= 8
    ro = jnp.where(edge, jnp.where(jnp.logical_or(slot == 8, slot == 11), 0, 1), slot // 4)
    j = jnp.where(edge, jnp.where(slot % 2 == 0, 4, -1), slot % 4)
    dy, dx = r - ro, i - j + 1
    ok = jnp.logical_and(jnp.logical_and(dy >= 0, dy < 3), jnp.logical_and(dx >= 0, dx < 3))
    idx = jnp.where(ok, 3 * dy + dx, -1)
    base = jnp.zeros((32, 384), F32)
    for d in range(9):
        base = jnp.where(idx == d, kt[d : d + 1], base)
    ps.sw[...] = jnp.zeros((288, 384), F32)
    for a in range(8):
        ps.sw[32 + a * 32 : 36 + a * 32] = base[4 * a : 4 * a + 4]
    for q in range(15):
        W["stem"][q] = ps.sw[32 - 2 * q : 288 - 2 * q].astype(BF)


def prep_plane(k, W, ch, ps):

    flat = jnp.concatenate([k[dy, dx] for dy in range(3) for dx in range(3)], axis=0)
    e = onehot(iota((128, ch), 0) % ch == iota((128, ch), 1))
    t = lax.dot_general(e, flat, (((1,), (1,)), ((), ())), preferred_element_type=F32).astype(BF)
    n = 9 * ch
    er, el = iota((n, 1152), 0), iota((n, 1152), 1)
    spread = onehot(jnp.logical_and(er // ch == el // 128, er % ch == el % ch))
    t = dot(t, spread).astype(BF)
    blocks = [[t[:, (3 * dy + dx) * 128 : (3 * dy + dx + 1) * 128] for dx in range(3)] for dy in range(3)]
    place_plane(blocks, W, ch)


def place_plane(blocks, W, ch, base=None):
    width = 128 // ch
    row, lane = iota((128, 128), 0), iota((128, 128), 1)
    i, j = row // ch, lane // ch
    zero = jnp.zeros((128, 128), F32)
    b32 = [[b.astype(F32) for b in q] for q in blocks]
    diag = []
    for dy in range(3):
        m = zero
        for dx in range(3):
            m = jnp.where(i - j + 1 == dx, b32[dy][dx], m)
        diag.append(m.astype(BF))
    zb = zero.astype(BF)

    def put(at, ro, v):
        if base is None:
            W[at : at + 128, ro * 128 : (ro + 1) * 128] = v
        else:
            W[base, at : at + 128, ro * 128 : (ro + 1) * 128] = v

    for r in range(4):
        for ro in range(2):
            put(r * 128, ro, diag[r - ro] if 0 <= r - ro < 3 else zb)

    def side(dy, dx):
        if not 0 <= dy < 3:
            return zero
        return jnp.where(j == (width - 1 if dx == 2 else 0), b32[dy][dx], 0.0)

    if ch == 32:
        for h in range(2):
            for ro in range(2):
                a, b = 2 * h - ro, 2 * h + 1 - ro
                v = jnp.where(i == 0, side(a, 2), jnp.where(i == 1, side(b, 0), jnp.where(i == 2, side(b, 2), side(a, 0))))
                put(512 + h * 128, ro, v.astype(BF))
    else:
        for r in range(4):
            for ro in range(2):
                v = jnp.where(i == 0, side(r - ro, 2), side(r - ro, 0))
                put(512 + r * 128, ro, v.astype(BF))


def prep_inner(k, W, ps):
    s = onehot(
        jnp.logical_and(iota((128, 256), 0) // 64 == iota((128, 256), 1) // 128,
                        iota((128, 256), 0) % 64 == iota((128, 256), 1) % 64)
    )
    ra, rl = iota((128, 64), 0), iota((128, 64), 1)
    a = onehot((ra % 64) == 2 * (rl % 32) + rl // 32)

    for zy in range(9):
        dz, dy = zy // 3, zy % 3
        at = (zy % 4) * 256
        for p in range(32):
            ps.st[at + p * 8 : at + p * 8 + 3] = k[dz, dy, :, p * 128 : (p + 1) * 128].astype(F32)
        for dx in range(3):
            d = 3 * zy + dx
            ps.ma[d * 32 : d * 32 + 32] = ps.st[pl.ds(at + dx, 32, 8), :].astype(BF)
    ps.mb[...] = dot(ps.ma[...], s).astype(BF)
    cols = [
        jnp.concatenate([ps.mb[d * 32 : d * 32 + 32, 0:128], ps.mb[d * 32 : d * 32 + 32, 128:256]], axis=0)
        for d in range(27)
    ]
    t = dot(a, jnp.concatenate(cols, axis=1)).astype(BF)
    for dz in range(3):
        blocks = [
            [t[:, (9 * dz + 3 * dy + dx) * 128 : (9 * dz + 3 * dy + dx + 1) * 128] for dx in range(3)]
            for dy in range(3)
        ]
        place_plane(blocks, W, 64, base=dz)


def prep_bottom(k, W, ps):
    zb = jnp.zeros((384, 128), BF)
    for dz in range(3):
        W[dz, 0:384, 128:256] = zb
        W[dz, 1152:1536, 0:128] = zb

    def plane(zy, _):
        dz = zy // 3
        dy = zy - 3 * dz
        for c in range(128):
            ps.st[c * 8 : c * 8 + 3] = k[dz, dy, :, c * 128 : (c + 1) * 128].astype(F32)
        for dx in range(3):
            m = ps.st[pl.ds(dx, 128, 8), :].astype(BF)
            W[dz, pl.ds(pl.multiple_of(dy * 384 + dx * 128, 128), 128), 0:128] = m
            W[dz, pl.ds(pl.multiple_of(dy * 384 + 384 + dx * 128, 128), 128), 128:256] = m
        return 0

    lax.fori_loop(0, 9, plane, 0)


def corners(k, ch, ps):
    n = k.shape[3]
    for c in range(ch):
        for p in range(2):
            v = k[c, p].astype(F32)
            ps.st[(2 * c + p) * 8 : (2 * c + p) * 8 + 2, 0:n] = v
    return [[ps.st[pl.ds(8 * p + q, ch, 16), :] for q in range(2)] for p in range(2)]


def prep_corners(raw, W, ps):
    lane = iota((32, 128), 1)
    for name in ("pool", "expand"):
        x = corners(raw[name], 32, ps)
        rows = []
        for p in range(2):
            for i in range(4):
                v = jnp.where(lane < 64, x[p][i % 2], 0.0)
                rows.append(v if i < 2 else pltpu.roll(v, 64, 1))
        z = jnp.concatenate(rows, axis=0)
        if name == "pool":
            W["pool"][...] = z.astype(BF)
        else:
            W["expand"][...] = jnp.concatenate([z[0:128].T, z[128:256].T], axis=1).astype(BF)
    x = corners(raw["narrow"], 64, ps)
    W["narrow"][...] = jnp.concatenate([x[p][q] for p in range(2) for q in range(2)], axis=0).astype(BF)
    x = corners(raw["lift"], 64, ps)
    z = [jnp.concatenate([x[p][0], x[p][1]], axis=0) for p in range(2)]
    W["lift"][...] = jnp.concatenate([z[0].T, z[1].T], axis=1).astype(BF)


def prep_head(raw, W):
    h = raw["head"][...].astype(F32)
    h = jnp.concatenate([h, h, jnp.zeros((2, 32), F32)], axis=0).astype(BF)
    e = onehot(iota((32, 256), 0) == iota((32, 256), 1) % 32)
    t = dot(h, e)
    row, lane = iota((8, 256), 0), iota((8, 256), 1)
    ro = jnp.where(row < 3, 0, 1)
    W["head"][...] = jnp.where(jnp.logical_and(row < 6, ro == lane // 128), t, 0.0).astype(BF)


def prep_all(raw, rawb, W, B, ps):
    prep_bias(rawb, B)
    prep_stem(raw, W, ps)
    prep_plane(raw["outer"], W["outer"], 32, ps)
    prep_corners(raw, W, ps)
    prep_inner(raw["inner"], W["inner"], ps)
    prep_bottom(raw["bottom"], W["bottom"], ps)
    prep_plane(raw["mend"], W["mend"], 64, ps)
    prep_plane(raw["finish"], W["finish"], 32, ps)
    prep_head(raw, W)


MESH = pl.DeviceIdType.MESH


def axis_position():
    return lax.axis_index("sec"), lax.axis_index("gy"), lax.axis_index("gx")


def align(own, left, right, has_left, has_right, cs):
    lane = lax.broadcasted_iota(jnp.int32, (1, 128), 1)

    def shifts(ref, first, ok):
        v = ref[64:80].astype(F32)
        m = jnp.concatenate([jnp.broadcast_to(v[first + i : first + i + 1], (8, 128)) for i in range(8)], axis=0)
        return m if ok is None else jnp.where(ok, m, -1.0)

    pix = [r[0:64].astype(F32) for r in (left, own, right)]
    oy = [shifts(left, 0, has_left), shifts(own, 0, None), shifts(right, 0, has_right)]
    ox = [shifts(left, 8, has_left), shifts(own, 8, None), shifts(right, 8, has_right)]
    rp = [pltpu.roll(p, 16, 1) for p in pix]
    for tile in range(2):
        raw = jnp.where(lane < 16, rp[tile], rp[tile + 1])
        oyt = jnp.where(lane < 16, oy[tile], oy[tile + 1])
        oxt = jnp.where(lane < 16, ox[tile], ox[tile + 1])
        for s in range(5):
            hit = oxt == float(s)
            v = jnp.where(hit, raw, 0.0)
            o = jnp.where(hit, oyt, -1.0)
            cs.vs[s, tile] = v if s == 0 else pltpu.roll(v, s, 1)
            cs.os[s, tile] = o if s == 0 else pltpu.roll(o, s, 1)
    cs.vb[:, :, 0:8] = jnp.zeros((2, 2, 8, 128), F32)
    for tile in range(2):
        total = jnp.zeros((64, 128), F32)
        cover = jnp.zeros((64, 128), F32)
        for t in range(5):
            v = jnp.zeros((64, 128), F32)
            c = jnp.zeros((64, 128), F32)
            for s in range(5):
                vs, os = cs.vs[s, tile], cs.os[s, tile]
                if tile == 1 and s > 0:
                    vs = jnp.where(lane < s, cs.vs[s, 0], vs)
                    os = jnp.where(lane < s, cs.os[s, 0], os)
                hit = os == float(t)
                v = v + jnp.where(hit, vs, 0.0)
                c = c + jnp.where(hit, 1.0, 0.0)
            if t > 0:
                cs.vb[tile, 0, 8:72] = v
                cs.vb[tile, 1, 8:72] = c
                v = cs.vb[tile, 0, 8 - t : 72 - t]
                c = cs.vb[tile, 1, 8 - t : 72 - t]
            total = total + v
            cover = cover + c
        a = (total / jnp.maximum(cover, 1.0)).astype(BF).astype(F32)
        if tile == 0:
            a = jnp.where(jnp.logical_or(lane >= 16, has_left), a, 0.0)
        else:
            a = jnp.where(jnp.logical_or(lane < 16, has_right), a, 0.0)
        a = jnp.concatenate([a, jnp.zeros((64, 128), F32)], axis=0)
        cs.tt[tile * 128 : (tile + 1) * 128] = a.T
    xs = [cs.tt[pl.ds(4 + i, 48, 4), :] for i in range(4)]
    for g in range(8):
        piece = jnp.zeros((48, 128), F32)
        for i in range(4):
            sh = (32 * i - (8 * g - 12)) % 128
            r = xs[i] if sh == 0 else pltpu.roll(xs[i], sh, 1)
            piece = jnp.where(lane // 32 == i, r, piece)
        cs.sbuf[g] = piece.astype(BF)


CS = dict(
    img=((64, 128), BF),
    off=((2, 8), jnp.int32),
    near=((80, 128), BF),
    rb=((2, 80, 128), BF),
    sbuf=((8, 48, 128), BF),
    rx=((NZ, 48, 128), BF),
    vs=((5, 2, 64, 128), F32),
    os=((5, 2, 64, 128), F32),
    vb=((2, 2, 72, 128), F32),
    tt=((256, 128), F32),
)


def gather(img_copy, off_copy, cs, sems, counts, first):
    send1, recv1, send2, send3, recv2 = sems
    sec, gy, gx = axis_position()
    nsec, ngy, ngx = counts
    one = jnp.int32(1)
    has_left, has_right = gx > 0, gx < ngx - 1
    above, below = sec > 0, sec < nsec - 1
    barrier = pltpu.get_barrier_semaphore()

    def greet(*device):
        pl.semaphore_signal(barrier, inc=1, device_id=device, device_id_type=MESH)

    cs.rx[...] = jnp.zeros((NZ, 48, 128), BF)
    cs.rb[...] = jnp.zeros((2, 80, 128), BF)

    @pl.when(has_left)
    def _():
        greet(sec, gy, gx - 1)

    @pl.when(has_right)
    def _():
        greet(sec, gy, gx + 1)

    for k in range(1, 8):
        greet(sec, lax.rem(gy + k, 8), gx)

    @pl.when(below)
    def _():
        greet(sec + 1, 0 * gy, gx)
        greet(sec + 1, 0 * gy + 1, gx)

    @pl.when(above)
    def _():
        greet(sec - 1, 0 * gy + 6, gx)
        greet(sec - 1, 0 * gy + 7, gx)

    to_up = jnp.logical_and(gy < 2, above)
    to_down = jnp.logical_and(gy >= 6, below)
    expect = 7 + jnp.where(has_left, 1, 0) + jnp.where(has_right, 1, 0) + jnp.where(jnp.logical_or(to_up, to_down), 8, 0)

    img_copy.wait()
    off_copy.wait()

    cs.near[0:64] = cs.img[...]
    sh = cs.off[...].astype(F32)
    r16 = iota((16, 8), 0)
    info = jnp.where(r16 < 8, sh[0:1], sh[1:2])
    info = jnp.sum(jnp.where(r16 % 8 == iota((16, 8), 1), info, 0.0), axis=1, keepdims=True)
    cs.near[64:80] = jnp.broadcast_to(info, (16, 128)).astype(BF)

    pl.semaphore_wait(barrier, expect)

    def near_copy(slot, target):
        return pltpu.make_async_remote_copy(
            src_ref=cs.near, dst_ref=cs.rb.at[slot], send_sem=send1.at[slot], recv_sem=recv1.at[slot],
            device_id=(sec, gy, target), device_id_type=MESH,
        )

    @pl.when(has_right)
    def _():
        near_copy(0, gx + 1).start()

    @pl.when(has_left)
    def _():
        near_copy(1, gx - 1).start()

    first()

    @pl.when(has_left)
    def _():
        near_copy(0, gx - 1).wait_recv()

    @pl.when(has_right)
    def _():
        near_copy(1, gx + 1).wait_recv()

    align(cs.near, cs.rb.at[0], cs.rb.at[1], has_left, has_right, cs)

    def far(g, slot, s, sem):
        return pltpu.make_async_remote_copy(
            src_ref=cs.sbuf.at[g], dst_ref=cs.rx.at[slot], send_sem=sem.at[g], recv_sem=recv2.at[slot],
            device_id=(s, g, gx), device_id_type=MESH,
        )

    for k in range(1, 8):
        far(lax.rem(gy + k, 8), gy + 2, sec, send2).start()

    @pl.when(to_up)
    def _():
        for k in range(8):
            far(lax.rem(gy + k, 8), gy + 10, sec - 1, send3).start()

    @pl.when(to_down)
    def _():
        for k in range(8):
            far(lax.rem(gy + k, 8), gy - 6, sec + 1, send3).start()

    cs.rx[gy + 2] = cs.sbuf[gy]

    def finish():
        for k in range(1, 8):
            far(lax.rem(gy + k, 8), 2 + lax.rem(gy + k, 8), sec, send2).wait_recv()

        @pl.when(above)
        def _():
            for slot in (0, 1):
                far(lax.rem(gy + 1, 8), slot, sec - 1, send3).wait_recv()

        @pl.when(below)
        def _():
            for slot in (10, 11):
                far(lax.rem(gy + 1, 8), slot, sec + 1, send3).wait_recv()

    def drain():
        @pl.when(has_right)
        def _():
            near_copy(0, gx + 1).wait_send()

        @pl.when(has_left)
        def _():
            near_copy(1, gx - 1).wait_send()

        for k in range(1, 8):
            far(lax.rem(gy + k, 8), gy + 2, sec, send2).wait_send()

        @pl.when(to_up)
        def _():
            for k in range(8):
                far(lax.rem(gy + k, 8), gy + 10, sec - 1, send3).wait_send()

        @pl.when(to_down)
        def _():
            for k in range(8):
                far(lax.rem(gy + k, 8), gy - 6, sec + 1, send3).wait_send()

    return finish, drain


def fused_call(images, offsets, raw, rawb, counts):
    nin = 2 + len(RAW) + len(RAWB)

    def body(*refs):
        ins, out, rest = refs[:nin], refs[nin], refs[nin + 1 :]

        def take(names):
            nonlocal rest
            head, rest = rest[: len(names)], rest[len(names) :]
            return head

        cs = Refs(CS, take(CS))
        sc = Refs(SCRATCH, take(SCRATCH))
        ps = Refs(PS, take(PS))
        W = dict(zip(WS, take(WS)))
        B = dict(zip(BS, take(BS)))
        R = dict(zip(RAW, take(RAW)))
        RB = dict(zip(RAWB, take(RAWB)))
        load = rest[0]
        sems = rest[1:]
        targets = [cs.img, cs.off] + list(R.values()) + list(RB.values())
        copies = [pltpu.make_async_copy(s, t, load.at[n]) for n, (s, t) in enumerate(zip(ins, targets))]
        for c in copies:
            c.start()

        def first():
            for c in copies[2:]:
                c.wait()
            prep_bias(RB, B)
            prep_stem(R, W, ps)
            prep_plane(R["outer"], W["outer"], 32, ps)

        finish, drain = gather(copies[0], copies[1], cs, sems, counts, first)
        prep_corners(R, W, ps)
        prep_inner(R["inner"], W["inner"], ps)
        prep_bottom(R["bottom"], W["bottom"], ps)
        prep_plane(R["mend"], W["mend"], 64, ps)
        prep_plane(R["finish"], W["finish"], 32, ps)
        prep_head(R, W)
        finish()
        drain()
        compute(axis_position(), counts, cs.rx, W, B, out, sc)

    dma = pltpu.SemaphoreType.DMA
    scratch = list(CS.values()) + list(SCRATCH.values()) + list(PS.values()) + list(WS.values())
    scratch += [(s, F32) for s in BS.values()] + [(s, BF) for s in RAW.values()]
    scratch += [((1, n), F32) for n in RAWB.values()]
    return pl.pallas_call(
        body,
        out_shape=jax.ShapeDtypeStruct((3, 8, 8, 128), F32),
        in_specs=[pl.BlockSpec(memory_space=pl.ANY)] * nin,
        out_specs=pl.BlockSpec(memory_space=pltpu.VMEM),
        scratch_shapes=[pltpu.VMEM(s, t) for s, t in scratch]
        + [dma((nin,)), dma((2,)), dma((2,)), dma((8,)), dma((8,)), dma((12,))],
        compiler_params=pltpu.CompilerParams(
            vmem_limit_bytes=62 * 1024 * 1024, collective_id=0, has_side_effects=True
        ),
    )(images, offsets, *[raw[k] for k in RAW], *[rawb[k] for k in RAWB])


NAMES = (
    "images", "offsets", "stem_kernel", "stem_bias", "outer_kernel", "outer_bias", "pooling_kernel",
    "pooling_bias", "inner_kernel", "inner_bias", "narrowing_kernel", "narrowing_bias", "bottom_kernel",
    "bottom_bias", "lift_kernel", "lift_bias", "mend_kernel", "mend_bias", "expand_kernel", "expand_bias",
    "finish_kernel", "finish_bias", "head_kernel", "head_bias",
)


def solution(mesh):
    counts = (mesh.shape["sec"], mesh.shape["gy"], mesh.shape["gx"])

    def per_device(*args):
        w = dict(zip(NAMES, args))
        raw, rawb = raw_views(w)
        offsets = w["offsets"][0, :, :, 0].T
        logits = fused_call(w["images"].reshape(64, 128), offsets, raw, rawb, counts)
        return jax.nn.sigmoid(logits + w["head_bias"][:, None, None, None])

    in_specs = (P(("sec", "gy"), None, "gx"), P(("sec", "gy"), None, None, "gx")) + (P(),) * 22
    out_specs = P(None, "sec", "gy", "gx")
    return jax.shard_map(per_device, mesh=mesh, in_specs=in_specs, out_specs=out_specs, check_vma=False)
```

```python
import jax
import jax.numpy as jnp
from jax import lax
from jax.experimental import pallas as pl
from jax.experimental.pallas import tpu as pltpu
from jax.sharding import PartitionSpec as P

BF = jnp.bfloat16
F32 = jnp.float32
PITCH = 40
NZ = 12
OUTER_GROUP, INNER_GROUP = 14, 3
R12, R10, R8 = NZ * PITCH, 10 * PITCH, 8 * PITCH
PAD = 16


WN = ("stem", "outer", "pool", "inner", "narrow", "bottom", "lift", "mend", "expand", "finish", "head")
BN = ("stem", "outer", "pool", "inner", "narrow", "bottom", "lift", "mend", "expand", "finish")


def dot(a, b):
    return jnp.dot(a, b, preferred_element_type=F32)


def setup(pos, counts, sc):
    sec, gy, gx = pos
    nsec, ngy, ngx = counts
    lane = lax.broadcasted_iota(jnp.int32, (1, 128), 1)
    rows = lax.broadcasted_iota(jnp.int32, (R12, 1), 0)
    zi = rows // PITCH
    gi = rows - zi * PITCH
    zglob = sec * 8 - 2 + zi
    zok = jnp.logical_and(zglob >= 0, zglob < nsec * 8)
    gg = gx * 32 - 3 + gi

    def gok(shift):
        return jnp.logical_and(gg + shift >= 0, gg + shift < ngx * 32)

    m = jnp.broadcast_to(jnp.where(jnp.logical_and(zok, gok(0)), 1.0, 0.0), (R12, 128))
    sc.mask[0] = jnp.zeros((R12, 128), F32)
    sc.mask[1] = m
    sc.smask[0] = jnp.zeros((R12, 128), BF)
    sc.smask[1] = m.astype(BF)
    right = jnp.where(gok(1), 1.0, 0.0)
    left = jnp.where(gok(-1), 1.0, 0.0)
    zero = jnp.zeros((R12, 1), F32)
    for va in range(2):
        for vb in range(2):
            ra, la = (right, left) if va else (zero, zero)
            rb, lb = (right, left) if vb else (zero, zero)
            e = jnp.where(lane < 32, ra, jnp.where(lane < 64, lb, jnp.where(lane < 96, rb, la)))
            sc.emask[2 * va + vb] = e.astype(BF)
    sc.xf[0:PAD] = jnp.zeros((PAD, 128), F32)
    sc.xf[PAD + R12 :] = jnp.zeros((PAD, 128), F32)
    sc.pf[:, 0:PAD] = jnp.zeros((14, PAD, 128), F32)
    sc.pf[:, PAD + R12 :] = jnp.zeros((14, PAD, 128), F32)
    sc.qf[:, 0:PAD] = jnp.zeros((6, PAD, 128), F32)
    sc.qf[:, PAD + R10 :] = jnp.zeros((6, PAD, 128), F32)
    sc.lf[:, 0:PAD] = jnp.zeros((8, PAD, 128), F32)
    sc.lf[:, PAD + R8 :] = jnp.zeros((8, PAD, 128), F32)


def compute(pos, counts, x4, W, B, out, sc):
    sec, gy, gx = pos
    nsec, ngy, ngx = counts
    lane = lax.broadcasted_iota(jnp.int32, (1, 128), 1)
    def rowok(row, total):
        return jnp.where(jnp.logical_and(row >= 0, row < total), 1, 0)

    for z in range(NZ):
        sc.xf[PAD + z * PITCH : PAD + (z + 1) * PITCH] = x4[z, 0:PITCH].astype(F32)
    sc.xin[:, 0:128] = sc.xf[PAD : PAD + R12].astype(BF)
    sc.xin[:, 128:256] = jnp.where(
        lane < 64, sc.xf[PAD + 1 : PAD + 1 + R12], sc.xf[PAD - 1 : PAD - 1 + R12]
    ).astype(BF)

    zero_bf = jnp.zeros((), BF)

    for q in range(15):
        acc = dot(sc.xin[...], W["stem"][q]) + B["stem"][...]
        s = acc.astype(BF)
        va = rowok(gy * 8 + 2 * q - 11, ngy * 8)
        vb = rowok(gy * 8 + 2 * q - 10, ngy * 8)
        sc.se[q] = s[:, 0:128]
        sc.so[q] = s[:, 128:256]
        r = jnp.maximum(s, zero_bf)
        sc.re[q] = r[:, 0:128] * sc.smask[va]
        sc.ro[q] = r[:, 128:256] * sc.smask[vb]
        sc.e[q] = r[:, 256:384] * sc.emask[2 * va + vb]

    def flat(ref, start, count, *rest):
        v = ref[(pl.ds(start, count),) + rest]
        return v.reshape(count * v.shape[1], v.shape[2])


    NP = OUTER_GROUP

    def outer(c, _):
        p = c * NP
        lhs = jnp.concatenate(
            [flat(x, p + h, NP) for h in range(2) for x in (sc.re, sc.ro)] + [flat(sc.e, p, NP), flat(sc.e, p + 1, NP)],
            axis=1,
        )
        acc = dot(lhs, W["outer"][...])
        res = jnp.concatenate([flat(sc.so, p, NP), flat(sc.se, p + 1, NP)], axis=1).astype(F32)
        o = (acc + res + B["outer"][...]).astype(BF)
        for i in range(NP):
            @pl.when(jnp.logical_and(p + i >= 4, p + i < 10))
            def _():
                sc.o[p + i - 4] = o[i * R12 + 80 : i * R12 + 400]
        pooled = (dot(o, W["pool"][...]) + B["pool"][...]).astype(BF).astype(F32)
        for i in range(NP):
            v = rowok(gy * 4 + p + i - 5, ngy * 4)
            sc.pf[p + i, PAD : PAD + R12] = pooled[i * R12 : (i + 1) * R12] * sc.mask[v]
        for i in range(NP):
            q = p + i
            relu = lambda v: jnp.maximum(v, 0.0).astype(BF)
            sc.pa[q, :, 0:128] = relu(sc.pf[q, PAD : PAD + R12])
            ea = jnp.where(lane < 64, sc.pf[q, PAD + 1 : PAD + 1 + R12], sc.pf[q, PAD - 1 : PAD - 1 + R12])
            sc.pa[q, :, 128:256] = relu(ea)
            sc.pb[q, :, 0:128] = relu(sc.pf[q, PAD - 8 : PAD + 8 + R12])
            eb = jnp.where(lane < 64, sc.pf[q, PAD - 7 : PAD + 9 + R12], sc.pf[q, PAD - 9 : PAD + 7 + R12])
            sc.pb[q, :, 128:256] = relu(eb)
        return 0

    lax.fori_loop(0, 14 // NP, outer, 0)


    NK = INNER_GROUP

    def rows4(get, count):
        return [jnp.concatenate([get(2 * k + r) for k in range(count)], axis=0) for r in range(4)]

    def inner(c, _):
        k0 = c * NK
        pieces = []
        for dz in range(3):
            src = (sc.pa, sc.pb, sc.pa)[dz]
            lo = (0, 48, 80)[dz]
            for half in range(2):
                pieces += rows4(
                    lambda t: src[2 * k0 + t, lo : lo + R10, half * 128 : half * 128 + 128], NK
                )
        acc = dot(jnp.concatenate(pieces, axis=1), W["inner"][...].reshape(3072, 256))
        res = jnp.concatenate(
            [
                jnp.concatenate([sc.pf[2 * (k0 + k) + 1 + h, PAD + 40 : PAD + 440] for k in range(NK)], axis=0)
                for h in range(2)
            ],
            axis=1,
        )
        a = (acc + res + B["inner"][...]).astype(BF)
        for k in range(NK):
            sc.i[k0 + k] = a[k * R10 : (k + 1) * R10].astype(F32)[40:360].astype(BF)
        sq = (dot(a, W["narrow"][...]) + B["narrow"][...]).astype(BF).astype(F32)
        for k in range(NK):
            v = rowok(gy * 2 + k0 + k - 2, ngy * 2)
            sc.qf[k0 + k, PAD : PAD + R10] = sq[k * R10 : (k + 1) * R10] * sc.mask[v, 40:440]
        for k in range(NK):
            for d in range(3):
                sc.qa[k0 + k, :, d * 128 : (d + 1) * 128] = jnp.maximum(
                    sc.qf[k0 + k, PAD - 1 + d : PAD - 1 + d + R10], 0.0
                ).astype(BF)
                sc.qb[k0 + k, :, d * 128 : (d + 1) * 128] = jnp.maximum(
                    sc.qf[k0 + k, PAD - 9 + d : PAD + 7 + d + R10], 0.0
                ).astype(BF)
        return 0

    lax.fori_loop(0, 6 // NK, inner, 0)


    pieces = []
    for dz in range(3):
        src = (sc.qa, sc.qb, sc.qa)[dz]
        lo = (0, 48, 80)[dz]
        pieces += rows4(lambda t: src[t, lo : lo + R8, :], 2)
    acc = dot(jnp.concatenate(pieces, axis=1), W["bottom"][...].reshape(4608, 256))
    res = jnp.concatenate(
        [jnp.concatenate([sc.qf[2 * k + 1 + h, PAD + 40 : PAD + 360] for k in range(2)], axis=0) for h in range(2)],
        axis=1,
    )
    a = (acc + res + B["bottom"][...]).astype(BF)
    a = jnp.concatenate([a[k * R8 : (k + 1) * R8, h * 128 : h * 128 + 128] for k in range(2) for h in range(2)], axis=0)
    up = dot(a, W["lift"][...])
    l = (up + flat(sc.i, 1, 4).astype(F32) + B["lift"][...]).astype(BF).astype(F32)
    for t in range(8):
        y, e = t // 2, t % 2
        v = rowok(gy * 4 + t - 2, ngy * 4)
        sc.lf[t, PAD : PAD + R8] = l[y * R8 : (y + 1) * R8, e * 128 : (e + 1) * 128] * sc.mask[v, 80:400]
    for t in range(8):
        sc.pa[t, 0:R8, 0:128] = jnp.maximum(sc.lf[t, PAD : PAD + R8], 0.0).astype(BF)
        ed = jnp.where(lane < 64, sc.lf[t, PAD + 1 : PAD + 1 + R8], sc.lf[t, PAD - 1 : PAD - 1 + R8])
        sc.pa[t, 0:R8, 128:256] = jnp.maximum(ed, 0.0).astype(BF)

    pieces = rows4(lambda t: sc.pa[t, 0:R8, 0:128], 3) + rows4(lambda t: sc.pa[t, 0:R8, 128:256], 3)
    acc = dot(jnp.concatenate(pieces, axis=1), W["mend"][...])
    res = jnp.concatenate(
        [jnp.concatenate([sc.lf[2 * k + 1 + h, PAD : PAD + R8] for k in range(3)], axis=0) for h in range(2)], axis=1
    )
    a = (acc + res + B["mend"][...]).astype(BF)
    a = jnp.concatenate([a[k * R8 : (k + 1) * R8, h * 128 : h * 128 + 128] for k in range(3) for h in range(2)], axis=0)
    up = dot(a, W["expand"][...])
    x = (up + flat(sc.o, 0, 6).astype(F32) + B["expand"][...]).astype(BF).astype(F32)
    for t in range(1, 11):
        j, e = t // 2, t % 2
        v = rowok(gy * 8 + t - 2, ngy * 8)
        xm = x[j * R8 : (j + 1) * R8, e * 128 : (e + 1) * 128] * sc.mask[v, 80:400]
        sc.pf[t, PAD : PAD + R8] = xm
        sc.re[t, 0:R8] = jnp.maximum(xm, 0.0).astype(BF)
    for u in range(5):
        ta, tb = 2 * u + 1, 2 * u + 2
        ua = jnp.where(lane < 64, sc.pf[ta, PAD + 1 : PAD + 1 + R8], sc.pf[ta, PAD - 1 : PAD - 1 + R8])
        ub = jnp.where(lane < 64, sc.pf[tb, PAD + 1 : PAD + 1 + R8], sc.pf[tb, PAD - 1 : PAD - 1 + R8])
        ub = pltpu.roll(ub, 64, 1)
        e = jnp.where(jnp.logical_and(lane >= 32, lane < 96), ub, ua)
        sc.e[u, 0:R8] = jnp.maximum(e, 0.0).astype(BF)

    pieces = rows4(lambda t: sc.re[t + 1, 0:R8], 4) + [flat(sc.e, 0, 4, slice(0, R8)), flat(sc.e, 1, 4, slice(0, R8))]
    acc = dot(jnp.concatenate(pieces, axis=1), W["finish"][...])
    res = jnp.concatenate(
        [jnp.concatenate([sc.pf[2 * k + 2 + h, PAD : PAD + R8] for k in range(4)], axis=0) for h in range(2)], axis=1
    )
    f = (acc + res + B["finish"][...]).astype(BF).astype(F32)
    for h in range(2):
        for u in range(4):
            sc.f[h, u] = f[u * R8 : (u + 1) * R8, h * 128 : (h + 1) * 128]
    for u in range(4):
        for h in range(2):
            for z in range(8):
                fz = sc.f[h, u, z * PITCH + 3 : z * PITCH + 35]
                for j in range(4):
                    sc.g[u % 2, h, pl.ds(z * 128 + j, 32, 4), :] = jnp.where(lane // 32 == j, fz, 0.0)
        gz = jnp.concatenate([sc.g[u % 2, h] for h in range(2)], axis=1).astype(BF)
        lt = lax.dot_general(W["head"][...], gz, (((1,), (1,)), ((), ())), preferred_element_type=F32)
        for z in range(8):
            for ro in range(2):
                for o in range(3):
                    out[o, z, 2 * u + ro : 2 * u + ro + 1, :] = lt[ro * 3 + o : ro * 3 + o + 1, z * 128 : z * 128 + 128]


SCRATCH = dict(
    mask=((2, R12, 128), F32),
    smask=((2, R12, 128), BF),
    emask=((4, R12, 128), BF),
    xf=((R12 + 2 * PAD, 128), F32),
    xin=((R12, 256), BF),
    se=((15, R12, 128), BF),
    so=((15, R12, 128), BF),
    re=((15, R12, 128), BF),
    ro=((15, R12, 128), BF),
    e=((15, R12, 128), BF),
    o=((6, R8, 256), BF),
    pf=((14, R12 + 2 * PAD, 128), F32),
    pa=((14, R12, 256), BF),
    pb=((14, R12 + 16, 256), BF),
    i=((6, R8, 256), BF),
    qf=((6, R10 + 2 * PAD, 128), F32),
    qa=((6, R10, 384), BF),
    qb=((6, R10 + 16, 384), BF),
    lf=((8, R8 + 2 * PAD, 128), F32),
    f=((2, 4, R8, 128), F32),
    g=((2, 2, 1024, 128), F32),
)


class Refs:
    def __init__(self, names, refs):
        for n, r in zip(names, refs):
            setattr(self, n, r)


WS = dict(
    stem=((15, 256, 384), BF),
    outer=((768, 256), BF),
    pool=((256, 128), BF),
    inner=((3, 1024, 256), BF),
    narrow=((256, 128), BF),
    bottom=((3, 1536, 256), BF),
    lift=((128, 256), BF),
    mend=((1024, 256), BF),
    expand=((128, 256), BF),
    finish=((768, 256), BF),
    head=((8, 256), BF),
)
BS = dict(
    stem=(1, 384), outer=(1, 256), pool=(1, 128), inner=(1, 256), narrow=(1, 128), bottom=(1, 256),
    lift=(1, 256), mend=(1, 256), expand=(1, 256), finish=(1, 256),
)
RAW = dict(
    stem=(3, 3, 32), outer=(3, 3, 32, 32), pool=(32, 2, 2, 64), inner=(3, 3, 3, 4096), narrow=(64, 2, 2, 128),
    bottom=(3, 3, 3, 16384), lift=(64, 2, 2, 128), mend=(3, 3, 64, 64), expand=(32, 2, 2, 64),
    finish=(3, 3, 32, 32), head=(3, 32),
)
RAWB = dict(stem=32, outer=32, pool=64, inner=64, narrow=128, bottom=128, lift=64, mend=64, expand=32, finish=32)
LONG = dict(
    stem="stem", outer="outer", pool="pooling", inner="inner", narrow="narrowing", bottom="bottom", lift="lift",
    mend="mend", expand="expand", finish="finish",
)
PS = dict(
    st=((128 * 8, 128), F32),
    sw=((288, 384), F32),
    ma=((864, 128), BF),
    mb=((864, 256), BF),
)


def raw_views(w):
    def plane(k):
        return k[:, :, 0].transpose(2, 3, 0, 1)

    def inward(k):
        return k[:, :, 0].transpose(1, 2, 3, 0)

    raw = dict(
        stem=w["stem_kernel"][:, 0, 0].transpose(1, 2, 0),
        outer=plane(w["outer_kernel"]), mend=plane(w["mend_kernel"]), finish=plane(w["finish_kernel"]),
        pool=inward(w["pooling_kernel"]), narrow=inward(w["narrowing_kernel"]),
        lift=inward(w["lift_kernel"]), expand=inward(w["expand_kernel"]),
        inner=w["inner_kernel"], bottom=w["bottom_kernel"], head=w["head_kernel"],
    )
    bias = {k: w[LONG[k] + "_bias"].reshape(1, -1) for k in RAWB}
    return raw, bias


def iota(shape, dim):
    return lax.broadcasted_iota(jnp.int32, shape, dim)


def onehot(cond):
    return jnp.where(cond, 1.0, 0.0).astype(BF)


def prep_bias(raw, B):
    for k, n in RAWB.items():
        v = raw[k][...]
        reps = BS[k][1] // n
        B[k][...] = v if reps == 1 else jnp.concatenate([v] * reps, axis=1)


def prep_stem(raw, W, ps):
    k = jnp.concatenate([raw["stem"][dy].astype(F32) for dy in range(3)] + [jnp.zeros((7, 32), F32)], axis=0)
    e = onehot(iota((32, 384), 0) == iota((32, 384), 1) % 32)
    kt = dot(k.astype(BF), e)
    row, lane = iota((32, 384), 0), iota((32, 384), 1)
    a, r, slot = row // 4, row % 4, lane // 32
    i = jnp.where(a < 6, a, a - 8)
    edge = slot >= 8
    ro = jnp.where(edge, jnp.where(jnp.logical_or(slot == 8, slot == 11), 0, 1), slot // 4)
    j = jnp.where(edge, jnp.where(slot % 2 == 0, 4, -1), slot % 4)
    dy, dx = r - ro, i - j + 1
    ok = jnp.logical_and(jnp.logical_and(dy >= 0, dy < 3), jnp.logical_and(dx >= 0, dx < 3))
    idx = jnp.where(ok, 3 * dy + dx, -1)
    base = jnp.zeros((32, 384), F32)
    for d in range(9):
        base = jnp.where(idx == d, kt[d : d + 1], base)
    ps.sw[...] = jnp.zeros((288, 384), F32)
    for a in range(8):
        ps.sw[32 + a * 32 : 36 + a * 32] = base[4 * a : 4 * a + 4]
    for q in range(15):
        W["stem"][q] = ps.sw[32 - 2 * q : 288 - 2 * q].astype(BF)


def prep_plane(k, W, ch, ps):

    flat = jnp.concatenate([k[dy, dx] for dy in range(3) for dx in range(3)], axis=0)
    e = onehot(iota((128, ch), 0) % ch == iota((128, ch), 1))
    t = lax.dot_general(e, flat, (((1,), (1,)), ((), ())), preferred_element_type=F32).astype(BF)
    n = 9 * ch
    er, el = iota((n, 1152), 0), iota((n, 1152), 1)
    spread = onehot(jnp.logical_and(er // ch == el // 128, er % ch == el % ch))
    t = dot(t, spread).astype(BF)
    blocks = [[t[:, (3 * dy + dx) * 128 : (3 * dy + dx + 1) * 128] for dx in range(3)] for dy in range(3)]
    place_plane(blocks, W, ch)


def place_plane(blocks, W, ch, base=None):
    width = 128 // ch
    row, lane = iota((128, 128), 0), iota((128, 128), 1)
    i, j = row // ch, lane // ch
    zero = jnp.zeros((128, 128), F32)
    b32 = [[b.astype(F32) for b in q] for q in blocks]
    diag = []
    for dy in range(3):
        m = zero
        for dx in range(3):
            m = jnp.where(i - j + 1 == dx, b32[dy][dx], m)
        diag.append(m.astype(BF))
    zb = zero.astype(BF)

    def put(at, ro, v):
        if base is None:
            W[at : at + 128, ro * 128 : (ro + 1) * 128] = v
        else:
            W[base, at : at + 128, ro * 128 : (ro + 1) * 128] = v

    for r in range(4):
        for ro in range(2):
            put(r * 128, ro, diag[r - ro] if 0 <= r - ro < 3 else zb)

    def side(dy, dx):
        if not 0 <= dy < 3:
            return zero
        return jnp.where(j == (width - 1 if dx == 2 else 0), b32[dy][dx], 0.0)

    if ch == 32:
        for h in range(2):
            for ro in range(2):
                a, b = 2 * h - ro, 2 * h + 1 - ro
                v = jnp.where(i == 0, side(a, 2), jnp.where(i == 1, side(b, 0), jnp.where(i == 2, side(b, 2), side(a, 0))))
                put(512 + h * 128, ro, v.astype(BF))
    else:
        for r in range(4):
            for ro in range(2):
                v = jnp.where(i == 0, side(r - ro, 2), side(r - ro, 0))
                put(512 + r * 128, ro, v.astype(BF))


def prep_inner(k, W, ps):
    s = onehot(
        jnp.logical_and(iota((128, 256), 0) // 64 == iota((128, 256), 1) // 128,
                        iota((128, 256), 0) % 64 == iota((128, 256), 1) % 64)
    )
    ra, rl = iota((128, 64), 0), iota((128, 64), 1)
    a = onehot((ra % 64) == 2 * (rl % 32) + rl // 32)

    for zy in range(9):
        dz, dy = zy // 3, zy % 3
        at = (zy % 4) * 256
        for p in range(32):
            ps.st[at + p * 8 : at + p * 8 + 3] = k[dz, dy, :, p * 128 : (p + 1) * 128].astype(F32)
        for dx in range(3):
            d = 3 * zy + dx
            ps.ma[d * 32 : d * 32 + 32] = ps.st[pl.ds(at + dx, 32, 8), :].astype(BF)
    ps.mb[...] = dot(ps.ma[...], s).astype(BF)
    cols = [
        jnp.concatenate([ps.mb[d * 32 : d * 32 + 32, 0:128], ps.mb[d * 32 : d * 32 + 32, 128:256]], axis=0)
        for d in range(27)
    ]
    t = dot(a, jnp.concatenate(cols, axis=1)).astype(BF)
    for dz in range(3):
        blocks = [
            [t[:, (9 * dz + 3 * dy + dx) * 128 : (9 * dz + 3 * dy + dx + 1) * 128] for dx in range(3)]
            for dy in range(3)
        ]
        place_plane(blocks, W, 64, base=dz)


def prep_bottom(k, W, ps):
    zb = jnp.zeros((384, 128), BF)
    for dz in range(3):
        W[dz, 0:384, 128:256] = zb
        W[dz, 1152:1536, 0:128] = zb

    def plane(zy, _):
        dz = zy // 3
        dy = zy - 3 * dz
        for c in range(128):
            ps.st[c * 8 : c * 8 + 3] = k[dz, dy, :, c * 128 : (c + 1) * 128].astype(F32)
        for dx in range(3):
            m = ps.st[pl.ds(dx, 128, 8), :].astype(BF)
            W[dz, pl.ds(pl.multiple_of(dy * 384 + dx * 128, 128), 128), 0:128] = m
            W[dz, pl.ds(pl.multiple_of(dy * 384 + 384 + dx * 128, 128), 128), 128:256] = m
        return 0

    lax.fori_loop(0, 9, plane, 0)


def corners(k, ch, ps):
    n = k.shape[3]
    for c in range(ch):
        for p in range(2):
            v = k[c, p].astype(F32)
            ps.st[(2 * c + p) * 8 : (2 * c + p) * 8 + 2, 0:n] = v
    return [[ps.st[pl.ds(8 * p + q, ch, 16), :] for q in range(2)] for p in range(2)]


def prep_corners(raw, W, ps):
    lane = iota((32, 128), 1)
    for name in ("pool", "expand"):
        x = corners(raw[name], 32, ps)
        rows = []
        for p in range(2):
            for i in range(4):
                v = jnp.where(lane < 64, x[p][i % 2], 0.0)
                rows.append(v if i < 2 else pltpu.roll(v, 64, 1))
        z = jnp.concatenate(rows, axis=0)
        if name == "pool":
            W["pool"][...] = z.astype(BF)
        else:
            W["expand"][...] = jnp.concatenate([z[0:128].T, z[128:256].T], axis=1).astype(BF)
    x = corners(raw["narrow"], 64, ps)
    W["narrow"][...] = jnp.concatenate([x[p][q] for p in range(2) for q in range(2)], axis=0).astype(BF)
    x = corners(raw["lift"], 64, ps)
    z = [jnp.concatenate([x[p][0], x[p][1]], axis=0) for p in range(2)]
    W["lift"][...] = jnp.concatenate([z[0].T, z[1].T], axis=1).astype(BF)


def prep_head(raw, W):
    h = raw["head"][...].astype(F32)
    h = jnp.concatenate([h, h, jnp.zeros((2, 32), F32)], axis=0).astype(BF)
    e = onehot(iota((32, 256), 0) == iota((32, 256), 1) % 32)
    t = dot(h, e)
    row, lane = iota((8, 256), 0), iota((8, 256), 1)
    ro = jnp.where(row < 3, 0, 1)
    W["head"][...] = jnp.where(jnp.logical_and(row < 6, ro == lane // 128), t, 0.0).astype(BF)


def prep_all(raw, rawb, W, B, ps):
    prep_bias(rawb, B)
    prep_stem(raw, W, ps)
    prep_plane(raw["outer"], W["outer"], 32, ps)
    prep_corners(raw, W, ps)
    prep_inner(raw["inner"], W["inner"], ps)
    prep_bottom(raw["bottom"], W["bottom"], ps)
    prep_plane(raw["mend"], W["mend"], 64, ps)
    prep_plane(raw["finish"], W["finish"], 32, ps)
    prep_head(raw, W)


MESH = pl.DeviceIdType.MESH


def axis_position():
    return lax.axis_index("sec"), lax.axis_index("gy"), lax.axis_index("gx")


def align(own, left, right, has_left, has_right, cs):
    lane = lax.broadcasted_iota(jnp.int32, (1, 128), 1)

    def shifts(ref, first, ok):
        v = ref[64:80].astype(F32)
        m = jnp.concatenate([jnp.broadcast_to(v[first + i : first + i + 1], (8, 128)) for i in range(8)], axis=0)
        return m if ok is None else jnp.where(ok, m, -1.0)

    pix = [r[0:64].astype(F32) for r in (left, own, right)]
    oy = [shifts(left, 0, has_left), shifts(own, 0, None), shifts(right, 0, has_right)]
    ox = [shifts(left, 8, has_left), shifts(own, 8, None), shifts(right, 8, has_right)]
    rp = [pltpu.roll(p, 16, 1) for p in pix]
    for tile in range(2):
        raw = jnp.where(lane < 16, rp[tile], rp[tile + 1])
        oyt = jnp.where(lane < 16, oy[tile], oy[tile + 1])
        oxt = jnp.where(lane < 16, ox[tile], ox[tile + 1])
        for s in range(5):
            hit = oxt == float(s)
            v = jnp.where(hit, raw, 0.0)
            o = jnp.where(hit, oyt, -1.0)
            cs.vs[s, tile] = v if s == 0 else pltpu.roll(v, s, 1)
            cs.os[s, tile] = o if s == 0 else pltpu.roll(o, s, 1)
    cs.vb[:, :, 0:8] = jnp.zeros((2, 2, 8, 128), F32)
    for tile in range(2):
        total = jnp.zeros((64, 128), F32)
        cover = jnp.zeros((64, 128), F32)
        for t in range(5):
            v = jnp.zeros((64, 128), F32)
            c = jnp.zeros((64, 128), F32)
            for s in range(5):
                vs, os = cs.vs[s, tile], cs.os[s, tile]
                if tile == 1 and s > 0:
                    vs = jnp.where(lane < s, cs.vs[s, 0], vs)
                    os = jnp.where(lane < s, cs.os[s, 0], os)
                hit = os == float(t)
                v = v + jnp.where(hit, vs, 0.0)
                c = c + jnp.where(hit, 1.0, 0.0)
            if t > 0:
                cs.vb[tile, 0, 8:72] = v
                cs.vb[tile, 1, 8:72] = c
                v = cs.vb[tile, 0, 8 - t : 72 - t]
                c = cs.vb[tile, 1, 8 - t : 72 - t]
            total = total + v
            cover = cover + c
        a = (total / jnp.maximum(cover, 1.0)).astype(BF).astype(F32)
        if tile == 0:
            a = jnp.where(jnp.logical_or(lane >= 16, has_left), a, 0.0)
        else:
            a = jnp.where(jnp.logical_or(lane < 16, has_right), a, 0.0)
        a = jnp.concatenate([a, jnp.zeros((64, 128), F32)], axis=0)
        cs.tt[tile * 128 : (tile + 1) * 128] = a.T
    xs = [cs.tt[pl.ds(4 + i, 48, 4), :] for i in range(4)]
    for g in range(8):
        piece = jnp.zeros((48, 128), F32)
        for i in range(4):
            sh = (32 * i - (8 * g - 12)) % 128
            r = xs[i] if sh == 0 else pltpu.roll(xs[i], sh, 1)
            piece = jnp.where(lane // 32 == i, r, piece)
        cs.sbuf[g] = piece.astype(BF)


CS = dict(
    img=((64, 128), BF),
    off=((2, 8), jnp.int32),
    near=((80, 128), BF),
    rb=((2, 80, 128), BF),
    sbuf=((8, 48, 128), BF),
    rx=((NZ, 48, 128), BF),
    vs=((5, 2, 64, 128), F32),
    os=((5, 2, 64, 128), F32),
    vb=((2, 2, 72, 128), F32),
    tt=((256, 128), F32),
)


def gather(img_copy, off_copy, cs, sems, counts, first):
    send1, recv1, send2, send3, recv2 = sems
    sec, gy, gx = axis_position()
    nsec, ngy, ngx = counts
    one = jnp.int32(1)
    has_left, has_right = gx > 0, gx < ngx - 1
    above, below = sec > 0, sec < nsec - 1
    barrier = pltpu.get_barrier_semaphore()

    def greet(*device):
        pl.semaphore_signal(barrier, inc=1, device_id=device, device_id_type=MESH)

    cs.rx[...] = jnp.zeros((NZ, 48, 128), BF)
    cs.rb[...] = jnp.zeros((2, 80, 128), BF)

    @pl.when(has_left)
    def _():
        greet(sec, gy, gx - 1)

    @pl.when(has_right)
    def _():
        greet(sec, gy, gx + 1)

    for k in range(1, 8):
        greet(sec, lax.rem(gy + k, 8), gx)

    @pl.when(below)
    def _():
        greet(sec + 1, 0 * gy, gx)
        greet(sec + 1, 0 * gy + 1, gx)

    @pl.when(above)
    def _():
        greet(sec - 1, 0 * gy + 6, gx)
        greet(sec - 1, 0 * gy + 7, gx)

    to_up = jnp.logical_and(gy < 2, above)
    to_down = jnp.logical_and(gy >= 6, below)
    expect = 7 + jnp.where(has_left, 1, 0) + jnp.where(has_right, 1, 0) + jnp.where(jnp.logical_or(to_up, to_down), 8, 0)

    img_copy.wait()
    off_copy.wait()

    cs.near[0:64] = cs.img[...]
    sh = cs.off[...].astype(F32)
    r16 = iota((16, 8), 0)
    info = jnp.where(r16 < 8, sh[0:1], sh[1:2])
    info = jnp.sum(jnp.where(r16 % 8 == iota((16, 8), 1), info, 0.0), axis=1, keepdims=True)
    cs.near[64:80] = jnp.broadcast_to(info, (16, 128)).astype(BF)

    pl.semaphore_wait(barrier, expect)

    def near_copy(slot, target):
        return pltpu.make_async_remote_copy(
            src_ref=cs.near, dst_ref=cs.rb.at[slot], send_sem=send1.at[slot], recv_sem=recv1.at[slot],
            device_id=(sec, gy, target), device_id_type=MESH,
        )

    @pl.when(has_right)
    def _():
        near_copy(0, gx + 1).start()

    @pl.when(has_left)
    def _():
        near_copy(1, gx - 1).start()

    first()

    @pl.when(has_left)
    def _():
        near_copy(0, gx - 1).wait_recv()

    @pl.when(has_right)
    def _():
        near_copy(1, gx + 1).wait_recv()

    align(cs.near, cs.rb.at[0], cs.rb.at[1], has_left, has_right, cs)

    def far(g, slot, s, sem):
        return pltpu.make_async_remote_copy(
            src_ref=cs.sbuf.at[g], dst_ref=cs.rx.at[slot], send_sem=sem.at[g], recv_sem=recv2.at[slot],
            device_id=(s, g, gx), device_id_type=MESH,
        )

    for k in range(1, 8):
        far(lax.rem(gy + k, 8), gy + 2, sec, send2).start()

    @pl.when(to_up)
    def _():
        for k in range(8):
            far(lax.rem(gy + k, 8), gy + 10, sec - 1, send3).start()

    @pl.when(to_down)
    def _():
        for k in range(8):
            far(lax.rem(gy + k, 8), gy - 6, sec + 1, send3).start()

    cs.rx[gy + 2] = cs.sbuf[gy]

    def finish():
        for k in range(1, 8):
            far(lax.rem(gy + k, 8), 2 + lax.rem(gy + k, 8), sec, send2).wait_recv()

        @pl.when(above)
        def _():
            for slot in (0, 1):
                far(lax.rem(gy + 1, 8), slot, sec - 1, send3).wait_recv()

        @pl.when(below)
        def _():
            for slot in (10, 11):
                far(lax.rem(gy + 1, 8), slot, sec + 1, send3).wait_recv()

    def drain():
        @pl.when(has_right)
        def _():
            near_copy(0, gx + 1).wait_send()

        @pl.when(has_left)
        def _():
            near_copy(1, gx - 1).wait_send()

        for k in range(1, 8):
            far(lax.rem(gy + k, 8), gy + 2, sec, send2).wait_send()

        @pl.when(to_up)
        def _():
            for k in range(8):
                far(lax.rem(gy + k, 8), gy + 10, sec - 1, send3).wait_send()

        @pl.when(to_down)
        def _():
            for k in range(8):
                far(lax.rem(gy + k, 8), gy - 6, sec + 1, send3).wait_send()

    return finish, drain


def fused_call(images, offsets, raw, rawb, counts):
    nin = 2 + len(RAW) + len(RAWB)

    def body(*refs):
        ins, out, rest = refs[:nin], refs[nin], refs[nin + 1 :]

        def take(names):
            nonlocal rest
            head, rest = rest[: len(names)], rest[len(names) :]
            return head

        cs = Refs(CS, take(CS))
        sc = Refs(SCRATCH, take(SCRATCH))
        ps = Refs(PS, take(PS))
        W = dict(zip(WS, take(WS)))
        B = dict(zip(BS, take(BS)))
        R = dict(zip(RAW, take(RAW)))
        RB = dict(zip(RAWB, take(RAWB)))
        load = rest[0]
        sems = rest[1:]
        targets = [cs.img, cs.off] + list(R.values()) + list(RB.values())
        copies = [pltpu.make_async_copy(s, t, load.at[n]) for n, (s, t) in enumerate(zip(ins, targets))]
        for c in copies:
            c.start()

        def first():
            for c in copies[2:]:
                c.wait()
            prep_bias(RB, B)
            prep_stem(R, W, ps)
            prep_plane(R["outer"], W["outer"], 32, ps)

        finish, drain = gather(copies[0], copies[1], cs, sems, counts, first)
        prep_corners(R, W, ps)
        prep_inner(R["inner"], W["inner"], ps)
        prep_bottom(R["bottom"], W["bottom"], ps)
        prep_plane(R["mend"], W["mend"], 64, ps)
        prep_plane(R["finish"], W["finish"], 32, ps)
        prep_head(R, W)
        setup(axis_position(), counts, sc)
        finish()
        compute(axis_position(), counts, cs.rx, W, B, out, sc)
        drain()

    dma = pltpu.SemaphoreType.DMA
    scratch = list(CS.values()) + list(SCRATCH.values()) + list(PS.values()) + list(WS.values())
    scratch += [(s, F32) for s in BS.values()] + [(s, BF) for s in RAW.values()]
    scratch += [((1, n), F32) for n in RAWB.values()]
    return pl.pallas_call(
        body,
        out_shape=jax.ShapeDtypeStruct((3, 8, 8, 128), F32),
        in_specs=[pl.BlockSpec(memory_space=pl.ANY)] * nin,
        out_specs=pl.BlockSpec(memory_space=pltpu.VMEM),
        scratch_shapes=[pltpu.VMEM(s, t) for s, t in scratch]
        + [dma((nin,)), dma((2,)), dma((2,)), dma((8,)), dma((8,)), dma((12,))],
        compiler_params=pltpu.CompilerParams(
            vmem_limit_bytes=62 * 1024 * 1024, collective_id=0, has_side_effects=True
        ),
    )(images, offsets, *[raw[k] for k in RAW], *[rawb[k] for k in RAWB])


NAMES = (
    "images", "offsets", "stem_kernel", "stem_bias", "outer_kernel", "outer_bias", "pooling_kernel",
    "pooling_bias", "inner_kernel", "inner_bias", "narrowing_kernel", "narrowing_bias", "bottom_kernel",
    "bottom_bias", "lift_kernel", "lift_bias", "mend_kernel", "mend_bias", "expand_kernel", "expand_bias",
    "finish_kernel", "finish_bias", "head_kernel", "head_bias",
)


def solution(mesh):
    counts = (mesh.shape["sec"], mesh.shape["gy"], mesh.shape["gx"])

    def per_device(*args):
        w = dict(zip(NAMES, args))
        raw, rawb = raw_views(w)
        offsets = w["offsets"][0, :, :, 0].T
        logits = fused_call(w["images"].reshape(64, 128), offsets, raw, rawb, counts)
        return jax.nn.sigmoid(logits + w["head_bias"][:, None, None, None])

    in_specs = (P(("sec", "gy"), None, "gx"), P(("sec", "gy"), None, None, "gx")) + (P(),) * 22
    out_specs = P(None, "sec", "gy", "gx")
    return jax.shard_map(per_device, mesh=mesh, in_specs=in_specs, out_specs=out_specs, check_vma=False)
```
